32 devices in a mesh: expert: 8 (over z, x), split: 2 (over y), replica: 2 (over core).
Axes of the slice: x: 2, y: 2, z: 4, core: 2. Of those that a mesh axis runs over, the one named last changes fastest.
Arguments:
- tokens: bfloat16 [2, 2048, 2048], P('replica', 'expert', 'split'), may hold values from -6 to 6
- grad_out: bfloat16 [2, 2048, 2048], P('replica', 'expert', 'split'), may hold values from -6 to 6
- expert_ids: int32 [2, 2048, 2], P('replica', 'expert'), may hold values from 0 to 7, all different within a row; in each aligned block of 256 rows (0 to 255, 256 to 511, ..., all dimensions but the last counted through in order) at most 128 rows name the same one
- route_probs: float32 [2, 2048, 2], P('replica', 'expert'), may hold values from 0.1 to 0.9
- w_gate: bfloat16 [2, 8, 2048, 512], P('replica', 'expert', None, 'split'), may hold values from -0.125 to 0.125
- w_up: bfloat16 [2, 8, 2048, 512], P('replica', 'expert', None, 'split'), may hold values from -0.125 to 0.125
- w_down: bfloat16 [2, 8, 512, 2048], P('replica', 'expert', 'split'), may hold values from -0.25 to 0.25
- mom_gate: bfloat16 [2, 8, 2048, 512], P('replica', 'expert', None, 'split'), may hold values from -24 to 24
- mom_up: bfloat16 [2, 8, 2048, 512], P('replica', 'expert', None, 'split'), may hold values from -24 to 24
Outputs:
- avg_gate_w: bfloat16 [8, 2048, 512], P('expert', None, 'split')
- avg_up_w: bfloat16 [8, 2048, 512], P('expert', None, 'split')
- avg_gate_m: bfloat16 [8, 2048, 512], P('expert', None, 'split')
- avg_up_m: bfloat16 [8, 2048, 512], P('expert', None, 'split')
- d_tokens: bfloat16 [2, 2048, 2048], P('replica', 'expert', 'split')
The draws below stay inside these ranges and needn't reach their ends.
Inputs may be any that keep to these rules, and one draw needn't show every extreme that they name: `expert_ids`: each token names two different experts; among the 256 tokens of one device no expert is named more than 128 times, a bound that some block reaches on some device in every draw.
All inputs are finite; a program needn't handle non-finite values.
Results may differ from the reference program's by a relative error of at most 0.0065.
Values may be sent and summed in bfloat16 or wider, within the bound.
A program may use at most 128 MiB of HBM per device.

```python
import math
import jax
import jax.numpy as jnp
import numpy as np
from jax import lax

D = 2048
FF = 512
TOK_DEV = 256
EXPERTS = 8
CAP = 128
TOKP = 2048
REPLICAS = 2
N_EXPERT = 8
N_REPLICA = 2


def block_levels(key, extent, shards, least, high):
    level, own = 1.0, jax.random.fold_in(key, 6)
    for position, shards_of in shards:
        steps = jnp.exp(jax.random.uniform(jax.random.fold_in(own, position), (shards_of,), jnp.float32, least / len(shards), high / len(shards)))
        level = level * jnp.repeat(steps, extent[position] // shards_of).reshape([-1 if axis == position else 1 for axis in range(len(extent))])
    return level


def shared_out(stream_key, own, number, rows, number_of, top, most, lean):
    sequence = jax.random.permutation(stream_key, number_of)
    crowded, usual = shares(number_of, rows * top, most, lean, True), shares(number_of, rows * top, most, lean, False)
    places = jnp.arange(number_of)

    def named(lengths, turn):
        used = int((lengths > 0).sum())
        fixed = max(1, used // 4)
        shifted = fixed + (places - fixed + turn * (used - fixed)) % max(1, number_of - fixed)
        return jnp.zeros((number_of,), jnp.int32).at[sequence[jnp.where(places < fixed, places, shifted)]].set(jnp.asarray(lengths, jnp.int32))

    lengths = jnp.where(number % 4 == 0, named(crowded, number // 4), named(usual, number - number // 4 - 1))
    mixed = jax.random.permutation(jax.random.fold_in(own, 3), number_of)
    giver, sink = mixed[0:number_of // 2 * 2:2], mixed[1:number_of // 2 * 2:2]
    room = jnp.minimum(lengths[giver] - 1, most - lengths[sink]) // 2
    room = jnp.where((giver == sequence[0]) | (sink == sequence[0]) | (lengths[sink] == 0), 0, jnp.maximum(room, 0))
    shifted = jax.random.randint(jax.random.fold_in(own, 4), (number_of // 2,), 0, 1 << 20) % (room + 1)
    lengths = lengths.at[giver].add(-shifted).at[sink].add(shifted)
    labels = jnp.searchsorted(jnp.cumsum(lengths), jnp.arange(rows * top), side="right").astype(jnp.int32)
    table = labels.reshape(top, rows).T
    table = table[jax.random.permutation(jax.random.fold_in(own, 1), rows)]
    turn = jax.random.randint(jax.random.fold_in(own, 2), (rows, 1), 0, top)
    return jnp.take_along_axis(table, (jnp.arange(top)[None, :] + turn) % top, axis=1)


def shares(count, total, reach, slope, full):
    loads = [(1 << 20) // math.isqrt(grade ** slope) + 1 for grade in range(1, count + 1)]
    largest = reach if full else min(reach, max(-(-total // count), total * loads[0] // sum(loads)))
    least = 1 if total - largest >= count - 1 else 0
    holding, rest = [largest] + [least] * (count - 1), total - largest - least * (count - 1)
    while rest > 0:
        movable = [i for i in range(1, count) if holding[i] < largest] or [i for i in range(1, count) if holding[i] < reach]
        whole, remaining = sum([loads[i] for i in movable]), rest
        for i in movable:
            addition = min(reach - holding[i], max(1, remaining * loads[i] // whole), rest)
            holding[i] = holding[i] + addition
            rest = rest - addition
    return np.array(holding)


def bell_draw(own_key, shape, deviation, limit, shards=(), held_as=jnp.bfloat16):
    result = deviation * jax.random.normal(own_key, shape, jnp.float32)
    if shards:
        result = result * block_levels(own_key, shape, shards, -0.22, 0.18)
    return jnp.clip(result, -limit, limit).astype(held_as)


def setup_inputs(seed: int = 0) -> dict:
    keys = jax.random.split(jax.random.key(seed), 10)
    tokens = bell_draw(keys[0], (REPLICAS, TOKP, D), 1.0, 6.0, ((0, 2), (1, 8), (2, 2)))
    grad_out = bell_draw(keys[1], (REPLICAS, TOKP, D), 1.0, 6.0, ((0, 2), (1, 8), (2, 2)))
    expert_ids_keys = jax.random.split(jax.random.fold_in(keys[2], 1), REPLICAS * TOKP // TOK_DEV)
    expert_ids_turns = jax.random.permutation(jax.random.fold_in(keys[2], 3), REPLICAS * TOKP // TOK_DEV)
    expert_ids = jax.vmap(lambda own, number: shared_out(jax.random.fold_in(keys[2], 2), own, number, TOK_DEV, EXPERTS, 2, CAP, 2))(expert_ids_keys, expert_ids_turns).reshape((REPLICAS, TOKP, 2))
    route_probs = jnp.clip(0.1 + 0.79999997 * jax.random.uniform(keys[3], (REPLICAS, TOKP, 2), jnp.float32) ** block_levels(keys[3], (REPLICAS, TOKP, 2), ((0, 2), (1, 8)), -0.2, 0.2), 0.1, 0.9)
    w_gate = bell_draw(keys[4], (REPLICAS, EXPERTS, D, FF), D ** -0.5, 0.125, ((0, 2), (1, 8), (3, 2)))
    w_up = bell_draw(keys[5], (REPLICAS, EXPERTS, D, FF), D ** -0.5, 0.125, ((0, 2), (1, 8), (3, 2)))
    w_down = bell_draw(keys[6], (REPLICAS, EXPERTS, FF, D), FF ** -0.5, 0.25, ((0, 2), (1, 8), (2, 2)))
    mom_gate = bell_draw(keys[7], (REPLICAS, EXPERTS, D, FF), 4.0, 24.0, ((0, 2), (1, 8), (3, 2)))
    mom_up = bell_draw(keys[8], (REPLICAS, EXPERTS, D, FF), 4.0, 24.0, ((0, 2), (1, 8), (3, 2)))
    return {"tokens": tokens, "grad_out": grad_out, "expert_ids": expert_ids, "route_probs": route_probs, "w_gate": w_gate, "w_up": w_up, "w_down": w_down, "mom_gate": mom_gate, "mom_up": mom_up}


momentum_decay = 0.9
step_size = 0.005


def slot_targets(ids_block, experts, capacity):
    flat_ids = ids_block.reshape(-1).astype(jnp.int32)
    onehot = (flat_ids[:, None] == jnp.arange(experts, dtype=jnp.int32)[None, :]).astype(jnp.int32)
    slot_rank = jnp.sum((jnp.cumsum(onehot, axis=0) - 1) * onehot, axis=1)
    return (flat_ids * capacity + slot_rank).astype(jnp.int32)


def expert_grads(rows_in, rows_out, gate_w, up_w, down_w):
    gate_pre = jnp.dot(rows_in, gate_w, preferred_element_type=jnp.float32)
    up_pre = jnp.dot(rows_in, up_w, preferred_element_type=jnp.float32)
    sigmoid_gate = jax.nn.sigmoid(gate_pre)
    activated = gate_pre * sigmoid_gate
    hidden_grad = lax.dot_general(rows_out, down_w, (((1,), (1,)), ((), ())), preferred_element_type=jnp.float32)
    d_up = (hidden_grad * activated).astype(jnp.bfloat16)
    d_gate = (hidden_grad * up_pre * sigmoid_gate * (1.0 + gate_pre * (1.0 - sigmoid_gate))).astype(jnp.bfloat16)
    g_gate = lax.dot_general(rows_in, d_gate, (((0,), (0,)), ((), ())), preferred_element_type=jnp.float32)
    g_up = lax.dot_general(rows_in, d_up, (((0,), (0,)), ((), ())), preferred_element_type=jnp.float32)
    d_rows = lax.dot_general(d_gate, gate_w, (((1,), (1,)), ((), ())), preferred_element_type=jnp.float32)
    d_rows = d_rows + lax.dot_general(d_up, up_w, (((1,), (1,)), ((), ())), preferred_element_type=jnp.float32)
    return g_gate, g_up, d_rows


def one_replica(packed):
    toks, grads, ids, probs, gate_w, up_w, down_w, gate_m, up_m = packed
    blocks = N_EXPERT
    experts = EXPERTS
    capacity = CAP
    targets = jax.vmap(lambda blk: slot_targets(blk, experts, capacity))(ids.reshape(blocks, TOK_DEV, 2))
    scaled = (grads[:, None, :].astype(jnp.float32) * probs[:, :, None]).astype(jnp.bfloat16)
    scaled = scaled.reshape(blocks, 2 * TOK_DEV, D)
    repeated = jnp.repeat(toks.reshape(blocks, TOK_DEV, D), 2, axis=1)

    def place(where, source):
        return jnp.zeros((experts * capacity, D), jnp.bfloat16).at[where].set(source)

    x_slots = jax.vmap(place)(targets, repeated).reshape(blocks, experts, capacity, D)
    y_slots = jax.vmap(place)(targets, scaled).reshape(blocks, experts, capacity, D)

    def per_expert(which):
        rows_in = x_slots[:, which].reshape(blocks * capacity, D)
        rows_out = y_slots[:, which].reshape(blocks * capacity, D)
        g_gate, g_up, d_rows = expert_grads(rows_in, rows_out, gate_w[which], up_w[which], down_w[which])
        return g_gate, g_up, d_rows.astype(jnp.bfloat16).reshape(blocks, capacity, D)

    g_gate, g_up, d_rows = lax.map(per_expert, jnp.arange(experts, dtype=jnp.int32))
    m_gate = momentum_decay * gate_m.astype(jnp.float32) + g_gate
    m_up = momentum_decay * up_m.astype(jnp.float32) + g_up
    new_gate = (gate_w.astype(jnp.float32) - step_size * m_gate).astype(jnp.bfloat16)
    new_up = (up_w.astype(jnp.float32) - step_size * m_up).astype(jnp.bfloat16)
    table = jnp.transpose(d_rows, (1, 0, 2, 3)).reshape(blocks, experts * capacity, D)
    picked = jax.vmap(lambda tab, where: tab[where])(table, targets)
    d_toks = picked.reshape(blocks, TOK_DEV, 2, D).astype(jnp.float32).sum(axis=2).astype(jnp.bfloat16)
    return new_gate, new_up, m_gate.astype(jnp.bfloat16), m_up.astype(jnp.bfloat16), d_toks.reshape(TOKP, D)


def reference(tokens, grad_out, expert_ids, route_probs, w_gate, w_up, w_down, mom_gate, mom_up):
    new_gate, new_up, m_gate, m_up, d_tokens = lax.map(
        one_replica, (tokens, grad_out, expert_ids, route_probs, w_gate, w_up, w_down, mom_gate, mom_up))

    def average(stack):
        return (jnp.sum(stack.astype(jnp.float32), axis=0) / N_REPLICA).astype(jnp.bfloat16)

    return average(new_gate), average(new_up), average(m_gate), average(m_up), d_tokens
```

```python
import functools

import jax
import jax.numpy as jnp
from jax import lax
from jax.experimental import pallas as pl
from jax.experimental.pallas import tpu as pltpu
from jax.sharding import PartitionSpec as P

momentum_decay = 0.9
step_size = 0.005
MESH = pl.DeviceIdType.MESH


def slot_targets(ids_block, experts, capacity):
    flat_ids = ids_block.reshape(-1)
    count = flat_ids.shape[0]
    place = jnp.arange(count, dtype=jnp.int32)
    same = (flat_ids[:, None] == flat_ids[None, :]) & (place[None, :] < place[:, None])
    return flat_ids * capacity + jnp.sum(same.astype(jnp.int32), axis=1)


def greet(axes):
    barrier = pltpu.get_barrier_semaphore()
    total = 0
    for name, size in axes:
        here = lax.axis_index(name)

        def signal(step, carry, name=name, size=size, here=here):
            pl.semaphore_signal(
                barrier, inc=1, device_id={name: lax.rem(here + step, size)}, device_id_type=MESH
            )
            return carry

        lax.fori_loop(1, size, signal, 0)
        total += size - 1
    pl.semaphore_wait(barrier, total)


def remote(src, dst, send, recv, name, to):
    return pltpu.make_async_remote_copy(
        src_ref=src, dst_ref=dst, send_sem=send, recv_sem=recv, device_id={name: to}, device_id_type=MESH
    )


def dispatch_kernel(
    experts, splits, pick_ref, scale_ref, tok_ref, grad_ref, in_ref, out_ref,
    slots, own_sem, send_sem, recv_sem, fsend_sem, frecv_sem,
):
    me = lax.axis_index("expert")
    part = lax.axis_index("split")
    width = tok_ref.shape[1]
    got = (in_ref, out_ref)

    def cols(which):
        return pl.ds(pl.multiple_of(which * width, width), width)

    def make(arr, e):
        source = tok_ref if arr == 0 else grad_ref
        rows = jnp.dot(pick_ref[e], source[...], preferred_element_type=jnp.float32)
        if arr == 1:
            rows = rows * scale_ref[e][:, :1]
        slots[arr, e] = rows.astype(jnp.bfloat16)

    def hop(arr, e, frm):
        return remote(
            slots.at[arr, e], got[arr].at[frm, :, cols(part)], send_sem.at[arr, e], recv_sem.at[arr, frm],
            "expert", e,
        )

    def pass_on(arr, block, s, turn, to, frm):
        return remote(
            block, got[arr].at[s, :, cols(frm)], fsend_sem.at[arr, turn, s], frecv_sem.at[arr, turn, s],
            "split", to,
        )

    def keep(arr):
        return pltpu.make_async_copy(slots.at[arr, me], got[arr].at[me, :, cols(part)], own_sem.at[arr])

    greet((("expert", experts), ("split", splits)))
    for arr in range(2):

        def start(step, carry, arr=arr):
            e = lax.rem(me + step, experts)
            make(arr, e)
            hop(arr, e, me).start()
            return carry

        lax.fori_loop(1, experts, start, 0)
        make(arr, me)
        keep(arr).start()
        for turn in range(1, splits):
            pass_on(arr, slots.at[arr, me], me, turn, lax.rem(part + turn, splits), part).start()
    for arr in range(2):

        def forward(step, carry, arr=arr):
            s = lax.rem(me - step + experts, experts)
            hop(arr, s, s).wait_recv()
            for turn in range(1, splits):
                pass_on(
                    arr, got[arr].at[s, :, cols(part)], s, turn, lax.rem(part + turn, splits), part
                ).start()
            return carry

        lax.fori_loop(1, experts, forward, 0)
    for arr in range(2):

        def finish(step, carry, arr=arr):
            e = lax.rem(me + step, experts)
            hop(arr, e, me).wait_send()
            return carry

        lax.fori_loop(1, experts, finish, 0)
        keep(arr).wait()

        def drain(s, carry, arr=arr):
            for turn in range(1, splits):
                frm = lax.rem(part - turn + splits, splits)
                to = lax.rem(part + turn, splits)
                copy = pass_on(arr, slots.at[arr, s], s, turn, to, frm)
                copy.wait_send()
                copy.wait_recv()
            return carry

        lax.fori_loop(0, experts, drain, 0)


def dispatch(pick, scale, tokens, grads, experts, splits):
    capacity, width = pick.shape[1], tokens.shape[1]
    shape = jax.ShapeDtypeStruct((experts, capacity, splits * width), jnp.bfloat16)
    turns = max(splits, 2)
    return pl.pallas_call(
        functools.partial(dispatch_kernel, experts, splits),
        out_shape=(shape, shape),
        in_specs=[pl.BlockSpec(memory_space=pltpu.VMEM)] * 4,
        out_specs=(pl.BlockSpec(memory_space=pl.ANY), pl.BlockSpec(memory_space=pl.ANY)),
        scratch_shapes=[
            pltpu.VMEM((2, experts, capacity, width), jnp.bfloat16),
            pltpu.SemaphoreType.DMA((2,)),
            pltpu.SemaphoreType.DMA((2, experts)),
            pltpu.SemaphoreType.DMA((2, experts)),
            pltpu.SemaphoreType.DMA((2, turns, experts)),
            pltpu.SemaphoreType.DMA((2, turns, experts)),
        ],
        compiler_params=pltpu.CompilerParams(
            collective_id=0, has_side_effects=True, vmem_limit_bytes=40 << 20
        ),
        name="dispatch",
    )(pick, scale, tokens, grads)


def back_kernel(
    experts, splits, replicas, grads_ref, weights_ref, a_ref, b_ref, c_ref, d_ref,
    home_ref, oa_ref, ob_ref, oc_ref, od_ref,
    away, landed, ready, xsend, xrecv, own_sem, send_sem, recv_sem, rsend, rrecv,
):
    me = lax.axis_index("expert")
    part = lax.axis_index("split")
    copy_of = lax.axis_index("replica")
    width = weights_ref.shape[0] // splits
    stepped = (a_ref, b_ref, c_ref, d_ref)
    others = (oa_ref, ob_ref, oc_ref, od_ref)

    def product(e, which):
        rows = pl.ds(pl.multiple_of(which * width, width), width)
        return lax.dot_general(
            grads_ref[e], weights_ref[rows, :], (((1,), (1,)), ((), ())),
            preferred_element_type=jnp.float32,
        )

    def swap(k, turn):
        return remote(
            stepped[k], others[k].at[turn - 1], rsend.at[k, turn], rrecv.at[k, turn],
            "replica", lax.rem(copy_of + turn, replicas),
        )

    def cross(e, turn):
        return remote(
            away.at[turn, e], landed.at[turn, e], xsend.at[turn, e], xrecv.at[turn, e],
            "split", lax.rem(part + turn, splits),
        )

    def hop(e, frm):
        return remote(ready.at[e], home_ref.at[frm], send_sem.at[e], recv_sem.at[frm], "expert", e)

    greet((("expert", experts), ("split", splits), ("replica", replicas)))

    def first(step, carry):
        e = lax.rem(me + step, experts)
        for turn in range(1, splits):
            away[turn, e] = product(e, lax.rem(part + turn, splits)).astype(jnp.bfloat16)
            cross(e, turn).start()
        return carry

    lax.fori_loop(1, experts + 1, first, 0)
    for k in range(4):
        for turn in range(1, replicas):
            swap(k, turn).start()

    def total(e):
        value = product(e, part)
        for turn in range(1, splits):
            cross(e, turn).wait_recv()
            value = value + landed[turn, e].astype(jnp.float32)
        ready[e] = value.astype(jnp.bfloat16)

    def second(step, carry):
        e = lax.rem(me + step, experts)
        total(e)
        hop(e, me).start()
        return carry

    lax.fori_loop(1, experts, second, 0)
    total(me)
    keep = pltpu.make_async_copy(ready.at[me], home_ref.at[me], own_sem.at[0])
    keep.start()

    def last(step, carry):
        hop(lax.rem(me + step, experts), me).wait_send()
        s = lax.rem(me - step + experts, experts)
        hop(s, s).wait_recv()
        return carry

    lax.fori_loop(1, experts, last, 0)

    def sent(e, carry):
        for turn in range(1, splits):
            cross(e, turn).wait_send()
        return carry

    lax.fori_loop(0, experts, sent, 0)
    keep.wait()
    for k in range(4):
        for turn in range(1, replicas):
            swap(k, turn).wait()


def send_back(grads, weights, stepped, experts, splits, replicas):
    capacity = grads.shape[1]
    width = weights.shape[0] // splits
    turns, copies = max(splits, 2), max(replicas, 2)
    held = jax.ShapeDtypeStruct((copies - 1,) + stepped[0].shape, jnp.bfloat16)
    anywhere = pl.BlockSpec(memory_space=pl.ANY)
    inside = pl.BlockSpec(memory_space=pltpu.VMEM)
    return pl.pallas_call(
        functools.partial(back_kernel, experts, splits, replicas),
        out_shape=(jax.ShapeDtypeStruct((experts, capacity, width), jnp.bfloat16),) + (held,) * 4,
        in_specs=[inside] * 2 + [anywhere] * 4,
        out_specs=(anywhere,) * 5,
        scratch_shapes=[
            pltpu.VMEM((turns, experts, capacity, width), jnp.bfloat16),
            pltpu.VMEM((turns, experts, capacity, width), jnp.bfloat16),
            pltpu.VMEM((experts, capacity, width), jnp.bfloat16),
            pltpu.SemaphoreType.DMA((turns, experts)),
            pltpu.SemaphoreType.DMA((turns, experts)),
            pltpu.SemaphoreType.DMA((1,)),
            pltpu.SemaphoreType.DMA((experts,)),
            pltpu.SemaphoreType.DMA((experts,)),
            pltpu.SemaphoreType.DMA((4, copies)),
            pltpu.SemaphoreType.DMA((4, copies)),
        ],
        compiler_params=pltpu.CompilerParams(
            collective_id=1, has_side_effects=True, vmem_limit_bytes=40 << 20
        ),
        name="send_back",
    )(grads, weights, *stepped)


def hidden_grads(rows_in, rows_out, gate_w, up_w, down_w):
    gate_pre = jnp.dot(rows_in, gate_w, preferred_element_type=jnp.float32)
    up_pre = jnp.dot(rows_in, up_w, preferred_element_type=jnp.float32)
    sigmoid_gate = jax.nn.sigmoid(gate_pre)
    activated = gate_pre * sigmoid_gate
    hidden_grad = lax.dot_general(
        rows_out, down_w, (((1,), (1,)), ((), ())), preferred_element_type=jnp.float32
    )
    d_up = (hidden_grad * activated).astype(jnp.bfloat16)
    d_gate = (hidden_grad * up_pre * sigmoid_gate * (1.0 + gate_pre * (1.0 - sigmoid_gate))).astype(
        jnp.bfloat16
    )
    g_gate = lax.dot_general(
        rows_in, d_gate, (((0,), (0,)), ((), ())), preferred_element_type=jnp.float32
    )
    g_up = lax.dot_general(
        rows_in, d_up, (((0,), (0,)), ((), ())), preferred_element_type=jnp.float32
    )
    return (g_gate, g_up, d_gate, d_up)


def per_device(tokens, grad_out, expert_ids, route_probs, w_gate, w_up, w_down, mom_gate, mom_up):
    experts, splits = lax.axis_size("expert"), lax.axis_size("split")
    replicas = lax.axis_size("replica")
    tok_count = tokens.shape[1]
    capacity = 4 * tok_count // experts
    targets = slot_targets(expert_ids[0], experts, capacity).reshape(tok_count, 2)
    slot = jnp.arange(experts * capacity, dtype=jnp.int32)
    hits = [slot[:, None] == targets[:, k][None, :] for k in range(2)]
    pick = (hits[0] | hits[1]).astype(jnp.bfloat16)
    probs = route_probs[0]
    scale = sum(jnp.sum(jnp.where(hits[k], probs[:, k][None, :], 0.0), axis=1) for k in range(2))
    scale = jnp.broadcast_to(scale.reshape(experts, capacity, 1), (experts, capacity, 128))
    recv_in, recv_out = dispatch(
        pick.reshape(experts, capacity, tok_count), scale, tokens[0], grad_out[0], experts, splits
    )
    row_count = experts * capacity
    full_width = recv_in.shape[2]
    gate_local = w_gate[0, 0]
    up_local = w_up[0, 0]
    g_gate, g_up, d_gate, d_up = hidden_grads(
        recv_in.reshape(row_count, full_width),
        recv_out.reshape(row_count, full_width),
        gate_local,
        up_local,
        w_down[0, 0],
    )
    m_gate = momentum_decay * mom_gate[0, 0].astype(jnp.float32) + g_gate
    m_up = momentum_decay * mom_up[0, 0].astype(jnp.float32) + g_up
    stepped = (
        (gate_local.astype(jnp.float32) - step_size * m_gate).astype(jnp.bfloat16),
        (up_local.astype(jnp.float32) - step_size * m_up).astype(jnp.bfloat16),
        m_gate.astype(jnp.bfloat16),
        m_up.astype(jnp.bfloat16),
    )
    returned, *others = send_back(
        jnp.concatenate([d_gate, d_up], axis=1).reshape(experts, capacity, -1),
        jnp.concatenate([gate_local, up_local], axis=1),
        stepped, experts, splits, replicas,
    )
    averaged = []
    for mine, rest in zip(stepped, others):
        total = mine.astype(jnp.float32)
        for turn in range(replicas - 1):
            total = total + rest[turn].astype(jnp.float32)
        averaged.append((total / replicas).astype(jnp.bfloat16)[None])
    d_toks = lax.dot_general(
        pick, returned.reshape(row_count, -1), (((0,), (0,)), ((), ())),
        preferred_element_type=jnp.float32,
    ).astype(jnp.bfloat16)
    return (averaged[0], averaged[1], averaged[2], averaged[3], d_toks[None])


def solution(mesh):
    return jax.shard_map(
        per_device,
        mesh=mesh,
        in_specs=(
            P("replica", "expert", "split"),
            P("replica", "expert", "split"),
            P("replica", "expert", None),
            P("replica", "expert", None),
            P("replica", "expert", None, "split"),
            P("replica", "expert", None, "split"),
            P("replica", "expert", "split", None),
            P("replica", "expert", None, "split"),
            P("replica", "expert", None, "split"),
        ),
        out_specs=(
            P("expert", None, "split"),
            P("expert", None, "split"),
            P("expert", None, "split"),
            P("expert", None, "split"),
            P("replica", "expert", "split"),
        ),
        check_vma=False,
    )
```

```python
import functools

import jax
import jax.numpy as jnp
from jax import lax
from jax.experimental import pallas as pl
from jax.experimental.pallas import tpu as pltpu
from jax.sharding import PartitionSpec as P

momentum_decay = 0.9
step_size = 0.005
MESH = pl.DeviceIdType.MESH


def slot_targets(ids_block, experts, capacity):
    flat_ids = ids_block.reshape(-1)
    count = flat_ids.shape[0]
    place = jnp.arange(count, dtype=jnp.int32)
    same = (flat_ids[:, None] == flat_ids[None, :]) & (place[None, :] < place[:, None])
    return flat_ids * capacity + jnp.sum(same.astype(jnp.int32), axis=1)


def greet(axes):
    barrier = pltpu.get_barrier_semaphore()
    total = 0
    for name, size in axes:
        here = lax.axis_index(name)

        def signal(step, carry, name=name, size=size, here=here):
            pl.semaphore_signal(
                barrier, inc=1, device_id={name: lax.rem(here + step, size)}, device_id_type=MESH
            )
            return carry

        lax.fori_loop(1, size, signal, 0)
        total += size - 1
    pl.semaphore_wait(barrier, total)


def remote(src, dst, send, recv, name, to):
    return pltpu.make_async_remote_copy(
        src_ref=src, dst_ref=dst, send_sem=send, recv_sem=recv, device_id={name: to}, device_id_type=MESH
    )


def near(half):
    me = lax.axis_index("expert")
    base = (me // half) * half
    return lambda step: base + lax.rem(me - base + step, half)


def dispatch_kernel(
    experts, splits, place_ref, prob_ref, tok_ref, grad_ref, down_ref, in_ref, hid_ref,
    far_place, far_prob, far_tok, far_grad, slots, rows, far_down, term_out, term_in,
    raw_send, raw_recv, own_sem, send_sem, recv_sem, fsend_sem, frecv_sem,
    dsend_sem, drecv_sem, tsend_sem, trecv_sem,
):
    half = experts // 2
    me = lax.axis_index("expert")
    part = lax.axis_index("split")
    base = (me // half) * half
    mine = me - base
    partner = lax.rem(me + half, experts)
    count, width = tok_ref.shape
    capacity = rows.shape[1]
    turns = range(1, splits)
    peer = near(half)

    def cols(which):
        return pl.ds(pl.multiple_of(which * width, width), width)

    def ahead(turn):
        return lax.rem(part + turn, splits)

    def behind(turn):
        return lax.rem(part - turn + splits, splits)

    def raw(k):
        src = (place_ref, prob_ref, tok_ref, grad_ref)[k]
        dst = (far_place, far_prob, far_tok, far_grad)[k]
        return remote(src, dst, raw_send.at[k], raw_recv.at[k], "expert", partner)

    def down(turn):
        return remote(
            down_ref.at[:, cols(ahead(turn))], far_down.at[turn],
            dsend_sem.at[turn], drecv_sem.at[turn], "split", ahead(turn),
        )

    def make(arr, blk, e):
        place = far_place if blk else place_ref
        prob = far_prob if blk else prob_ref
        source = ((tok_ref, far_tok), (grad_ref, far_grad))[arr][blk]
        slot = lax.broadcasted_iota(jnp.int32, (capacity, count), 0) + e * capacity
        first, second = slot == place[0:1, :], slot == place[1:2, :]
        pick = jnp.where(first | second, 1.0, 0.0).astype(jnp.bfloat16)
        value = jnp.dot(pick, source[...], preferred_element_type=jnp.float32)
        if arr == 1:
            scale = jnp.where(first, prob[0:1, :], 0.0) + jnp.where(second, prob[1:2, :], 0.0)
            value = value * jnp.sum(scale, axis=1, keepdims=True)
        return value.astype(jnp.bfloat16)

    def landing(arr, s):
        return in_ref.at[s, :, cols(part)] if arr == 0 else rows.at[s]

    def hop(arr, blk, e, s):
        return remote(
            slots.at[arr, blk, e - base], landing(arr, s), send_sem.at[arr, blk, e - base],
            recv_sem.at[arr, s], "expert", e,
        )

    def pass_on(block, s, turn, frm):
        return remote(
            block, in_ref.at[s, :, cols(frm)], fsend_sem.at[turn, s], frecv_sem.at[turn, s],
            "split", ahead(turn),
        )

    def term(s, turn):
        return remote(
            term_out.at[turn, s], term_in.at[turn, s], tsend_sem.at[turn, s], trecv_sem.at[turn, s],
            "split", behind(turn),
        )

    def keep(blk, s):
        return pltpu.make_async_copy(slots.at[0, blk, mine], in_ref.at[s, :, cols(part)], own_sem.at[blk])

    def over(n0, n1, body):
        def run(i, carry):
            body(i)
            return carry

        lax.fori_loop(n0, n1, run, 0)

    def send_rows(arr, blk):
        s = partner if blk else me

        def one(step):
            e = peer(step)
            slots[arr, blk, e - base] = make(arr, blk, e)
            hop(arr, blk, e, s).start()

        over(1, half, one)
        if arr == 0:
            slots[0, blk, mine] = make(0, blk, me)
            keep(blk, s).start()
            for turn in turns:
                pass_on(slots.at[0, blk, mine], s, turn, part).start()
        else:
            rows[s] = make(1, blk, me)

    def other(step, blk):
        e = peer(half - step)
        return lax.rem(e + half, experts) if blk else e

    def forward(blk):
        def one(step):
            s = other(step, blk)
            hop(0, blk, peer(half - step), s).wait_recv()
            for turn in turns:
                pass_on(in_ref.at[s, :, cols(part)], s, turn, part).start()

        over(1, half, one)

    def terms(s):
        for turn in turns:
            value = lax.dot_general(
                rows[s], far_down[turn], (((1,), (1,)), ((), ())), preferred_element_type=jnp.float32
            )
            term_out[turn, s] = value.astype(jnp.bfloat16)
            term(s, turn).start()

    def use(blk):
        terms(partner if blk else me)

        def one(step):
            s = other(step, blk)
            hop(1, blk, peer(half - step), s).wait_recv()
            terms(s)

        over(1, half, one)

    barrier = pltpu.get_barrier_semaphore()
    over(1, half, lambda step: pl.semaphore_signal(
        barrier, inc=1, device_id={"expert": peer(step)}, device_id_type=MESH))
    pl.semaphore_signal(barrier, inc=1, device_id={"expert": partner}, device_id_type=MESH)
    for turn in turns:
        pl.semaphore_signal(barrier, inc=1, device_id={"split": ahead(turn)}, device_id_type=MESH)
    pl.semaphore_wait(barrier, half - 1 + 1 + splits - 1)

    for k in range(4):
        raw(k).start()
    send_rows(0, 0)
    for turn in turns:
        down(turn).start()
    send_rows(1, 0)
    forward(0)
    for k in range(3):
        raw(k).wait_recv()
    send_rows(0, 1)
    for turn in turns:
        down(turn).wait_recv()
    use(0)
    raw(3).wait_recv()
    send_rows(1, 1)
    forward(1)
    use(1)

    def finish(s):
        value = lax.dot_general(
            rows[s], down_ref[:, cols(part)], (((1,), (1,)), ((), ())),
            preferred_element_type=jnp.float32,
        )
        for turn in turns:
            copy = term(s, turn)
            copy.wait_send()
            copy.wait_recv()
            value = value + term_in[turn, s].astype(jnp.float32)
        hid_ref[s] = value

    over(0, experts, finish)

    def drain(s):
        for turn in turns:
            copy = pass_on(slots.at[0, 0, 0], s, turn, behind(turn))
            copy.wait_send()
            copy.wait_recv()

    over(0, experts, drain)
    for blk in range(2):
        for arr in range(2):
            over(1, half, lambda step: hop(arr, blk, peer(step), me).wait_send())
        keep(blk, partner if blk else me).wait()
    for k in range(4):
        raw(k).wait_send()
    for turn in turns:
        down(turn).wait_send()


def dispatch(place, probs, tokens, grads, down_w, experts, splits, capacity):
    count, width = tokens.shape
    hidden = down_w.shape[0]
    half, turns = experts // 2, max(splits, 2)
    bf16, dma = jnp.bfloat16, pltpu.SemaphoreType.DMA
    inside = pl.BlockSpec(memory_space=pltpu.VMEM)
    return pl.pallas_call(
        functools.partial(dispatch_kernel, experts, splits),
        out_shape=(
            jax.ShapeDtypeStruct((experts, capacity, splits * width), bf16),
            jax.ShapeDtypeStruct((experts, capacity, hidden), jnp.float32),
        ),
        in_specs=[inside] * 5,
        out_specs=(pl.BlockSpec(memory_space=pl.ANY), inside),
        scratch_shapes=[
            pltpu.VMEM(place.shape, jnp.int32),
            pltpu.VMEM(probs.shape, jnp.float32),
            pltpu.VMEM((count, width), bf16),
            pltpu.VMEM((count, width), bf16),
            pltpu.VMEM((2, 2, half, capacity, width), bf16),
            pltpu.VMEM((experts, capacity, width), bf16),
            pltpu.VMEM((turns, hidden, width), bf16),
            pltpu.VMEM((turns, experts, capacity, hidden), bf16),
            pltpu.VMEM((turns, experts, capacity, hidden), bf16),
            dma((4,)),
            dma((4,)),
            dma((2,)),
            dma((2, 2, half)),
            dma((2, experts)),
            dma((turns, experts)),
            dma((turns, experts)),
            dma((turns,)),
            dma((turns,)),
            dma((turns, experts)),
            dma((turns, experts)),
        ],
        compiler_params=pltpu.CompilerParams(
            collective_id=0, has_side_effects=True, vmem_limit_bytes=40 << 20
        ),
        name="dispatch",
    )(place, probs, tokens, grads, down_w)


def back_kernel(
    experts, splits, replicas, grads_ref, weights_ref, a_ref, b_ref, c_ref, d_ref,
    home_ref, oa_ref, ob_ref, oc_ref, od_ref,
    away, landed, ready, xsend, xrecv, own_sem, send_sem, recv_sem, rsend, rrecv,
):
    me = lax.axis_index("expert")
    part = lax.axis_index("split")
    copy_of = lax.axis_index("replica")
    width = weights_ref.shape[0] // splits
    stepped = (a_ref, b_ref, c_ref, d_ref)
    others = (oa_ref, ob_ref, oc_ref, od_ref)

    def product(e, which):
        rows = pl.ds(pl.multiple_of(which * width, width), width)
        return lax.dot_general(
            grads_ref[e], weights_ref[rows, :], (((1,), (1,)), ((), ())),
            preferred_element_type=jnp.float32,
        )

    def swap(k, turn):
        return remote(
            stepped[k], others[k].at[turn - 1], rsend.at[k, turn], rrecv.at[k, turn],
            "replica", lax.rem(copy_of + turn, replicas),
        )

    def cross(e, turn):
        return remote(
            away.at[turn, e], landed.at[turn, e], xsend.at[turn, e], xrecv.at[turn, e],
            "split", lax.rem(part + turn, splits),
        )

    def hop(e, frm):
        return remote(ready.at[e], home_ref.at[frm], send_sem.at[e], recv_sem.at[frm], "expert", e)

    greet((("expert", experts), ("split", splits), ("replica", replicas)))

    def first(step, carry):
        e = lax.rem(me + step, experts)
        for turn in range(1, splits):
            away[turn, e] = product(e, lax.rem(part + turn, splits)).astype(jnp.bfloat16)
            cross(e, turn).start()
        return carry

    lax.fori_loop(1, experts + 1, first, 0)
    for k in range(4):
        for turn in range(1, replicas):
            swap(k, turn).start()

    def total(e):
        value = product(e, part)
        for turn in range(1, splits):
            cross(e, turn).wait_recv()
            value = value + landed[turn, e].astype(jnp.float32)
        ready[e] = value.astype(jnp.bfloat16)

    def second(step, carry):
        e = lax.rem(me + step, experts)
        total(e)
        hop(e, me).start()
        return carry

    lax.fori_loop(1, experts, second, 0)
    total(me)
    keep = pltpu.make_async_copy(ready.at[me], home_ref.at[me], own_sem.at[0])
    keep.start()

    def last(step, carry):
        hop(lax.rem(me + step, experts), me).wait_send()
        s = lax.rem(me - step + experts, experts)
        hop(s, s).wait_recv()
        return carry

    lax.fori_loop(1, experts, last, 0)

    def sent(e, carry):
        for turn in range(1, splits):
            cross(e, turn).wait_send()
        return carry

    lax.fori_loop(0, experts, sent, 0)
    keep.wait()
    for k in range(4):
        for turn in range(1, replicas):
            swap(k, turn).wait()


def send_back(grads, weights, stepped, experts, splits, replicas):
    capacity = grads.shape[1]
    width = weights.shape[0] // splits
    turns, copies = max(splits, 2), max(replicas, 2)
    held = jax.ShapeDtypeStruct((copies - 1,) + stepped[0].shape, jnp.bfloat16)
    anywhere = pl.BlockSpec(memory_space=pl.ANY)
    inside = pl.BlockSpec(memory_space=pltpu.VMEM)
    return pl.pallas_call(
        functools.partial(back_kernel, experts, splits, replicas),
        out_shape=(jax.ShapeDtypeStruct((experts, capacity, width), jnp.bfloat16),) + (held,) * 4,
        in_specs=[inside] * 2 + [anywhere] * 4,
        out_specs=(anywhere,) * 5,
        scratch_shapes=[
            pltpu.VMEM((turns, experts, capacity, width), jnp.bfloat16),
            pltpu.VMEM((turns, experts, capacity, width), jnp.bfloat16),
            pltpu.VMEM((experts, capacity, width), jnp.bfloat16),
            pltpu.SemaphoreType.DMA((turns, experts)),
            pltpu.SemaphoreType.DMA((turns, experts)),
            pltpu.SemaphoreType.DMA((1,)),
            pltpu.SemaphoreType.DMA((experts,)),
            pltpu.SemaphoreType.DMA((experts,)),
            pltpu.SemaphoreType.DMA((4, copies)),
            pltpu.SemaphoreType.DMA((4, copies)),
        ],
        compiler_params=pltpu.CompilerParams(
            collective_id=1, has_side_effects=True, vmem_limit_bytes=40 << 20
        ),
        name="send_back",
    )(grads, weights, *stepped)


def hidden_grads(rows_in, hidden_grad, gate_w, up_w):
    gate_pre = jnp.dot(rows_in, gate_w, preferred_element_type=jnp.float32)
    up_pre = jnp.dot(rows_in, up_w, preferred_element_type=jnp.float32)
    sigmoid_gate = jax.nn.sigmoid(gate_pre)
    activated = gate_pre * sigmoid_gate
    d_up = (hidden_grad * activated).astype(jnp.bfloat16)
    d_gate = (hidden_grad * up_pre * sigmoid_gate * (1.0 + gate_pre * (1.0 - sigmoid_gate))).astype(
        jnp.bfloat16
    )
    g_gate = lax.dot_general(
        rows_in, d_gate, (((0,), (0,)), ((), ())), preferred_element_type=jnp.float32
    )
    g_up = lax.dot_general(
        rows_in, d_up, (((0,), (0,)), ((), ())), preferred_element_type=jnp.float32
    )
    return (g_gate, g_up, d_gate, d_up)


def per_device(tokens, grad_out, expert_ids, route_probs, w_gate, w_up, w_down, mom_gate, mom_up):
    experts, splits = lax.axis_size("expert"), lax.axis_size("split")
    replicas = lax.axis_size("replica")
    tok_count = tokens.shape[1]
    capacity = 4 * tok_count // experts
    targets = slot_targets(expert_ids[0], experts, capacity).reshape(tok_count, 2)
    slot = jnp.arange(experts * capacity, dtype=jnp.int32)
    hits = [slot[:, None] == targets[:, k][None, :] for k in range(2)]
    pick = (hits[0] | hits[1]).astype(jnp.bfloat16)
    probs = route_probs[0]
    place = jnp.pad(targets.T, ((0, 6), (0, 0)))
    recv_in, hidden_grad = dispatch(
        place, jnp.pad(probs.T, ((0, 6), (0, 0))), tokens[0], grad_out[0], w_down[0, 0],
        experts, splits, capacity,
    )
    row_count = experts * capacity
    full_width = recv_in.shape[2]
    gate_local = w_gate[0, 0]
    up_local = w_up[0, 0]
    g_gate, g_up, d_gate, d_up = hidden_grads(
        recv_in.reshape(row_count, full_width),
        hidden_grad.reshape(row_count, -1),
        gate_local,
        up_local,
    )
    m_gate = momentum_decay * mom_gate[0, 0].astype(jnp.float32) + g_gate
    m_up = momentum_decay * mom_up[0, 0].astype(jnp.float32) + g_up
    stepped = (
        (gate_local.astype(jnp.float32) - step_size * m_gate).astype(jnp.bfloat16),
        (up_local.astype(jnp.float32) - step_size * m_up).astype(jnp.bfloat16),
        m_gate.astype(jnp.bfloat16),
        m_up.astype(jnp.bfloat16),
    )
    returned, *others = send_back(
        jnp.concatenate([d_gate, d_up], axis=1).reshape(experts, capacity, -1),
        jnp.concatenate([gate_local, up_local], axis=1),
        stepped, experts, splits, replicas,
    )
    averaged = []
    for mine, rest in zip(stepped, others):
        total = mine.astype(jnp.float32)
        for turn in range(replicas - 1):
            total = total + rest[turn].astype(jnp.float32)
        averaged.append((total / replicas).astype(jnp.bfloat16)[None])
    d_toks = lax.dot_general(
        pick, returned.reshape(row_count, -1), (((0,), (0,)), ((), ())),
        preferred_element_type=jnp.float32,
    ).astype(jnp.bfloat16)
    return (averaged[0], averaged[1], averaged[2], averaged[3], d_toks[None])


def solution(mesh):
    return jax.shard_map(
        per_device,
        mesh=mesh,
        in_specs=(
            P("replica", "expert", "split"),
            P("replica", "expert", "split"),
            P("replica", "expert", None),
            P("replica", "expert", None),
            P("replica", "expert", None, "split"),
            P("replica", "expert", None, "split"),
            P("replica", "expert", "split", None),
            P("replica", "expert", None, "split"),
            P("replica", "expert", None, "split"),
        ),
        out_specs=(
            P("expert", None, "split"),
            P("expert", None, "split"),
            P("expert", None, "split"),
            P("expert", None, "split"),
            P("replica", "expert", "split"),
        ),
        check_vma=False,
    )
```

```python
import functools

import jax
import jax.numpy as jnp
from jax import lax
from jax.experimental import pallas as pl
from jax.experimental.pallas import tpu as pltpu
from jax.sharding import PartitionSpec as P

momentum_decay = 0.9
step_size = 0.005
MESH = pl.DeviceIdType.MESH


def slot_targets(ids_block, experts, capacity):
    flat_ids = ids_block.reshape(-1)
    count = flat_ids.shape[0]
    place = jnp.arange(count, dtype=jnp.int32)
    same = (flat_ids[:, None] == flat_ids[None, :]) & (place[None, :] < place[:, None])
    return flat_ids * capacity + jnp.sum(same.astype(jnp.int32), axis=1)


def greet(axes):
    barrier = pltpu.get_barrier_semaphore()
    total = 0
    for name, size in axes:
        here = lax.axis_index(name)

        def signal(step, carry, name=name, size=size, here=here):
            pl.semaphore_signal(
                barrier, inc=1, device_id={name: lax.rem(here + step, size)}, device_id_type=MESH
            )
            return carry

        lax.fori_loop(1, size, signal, 0)
        total += size - 1
    pl.semaphore_wait(barrier, total)


def remote(src, dst, send, recv, name, to):
    return pltpu.make_async_remote_copy(
        src_ref=src, dst_ref=dst, send_sem=send, recv_sem=recv, device_id={name: to}, device_id_type=MESH
    )


def near(half):
    me = lax.axis_index("expert")
    base = (me // half) * half
    return lambda step: base + lax.rem(me - base + step, half)


def dispatch_kernel(
    experts, splits, place_ref, prob_ref, tok_ref, grad_ref, down_ref, gate_ref, up_ref,
    in_ref, dgate_ref, dup_ref,
    far_place, far_prob, far_tok, far_grad, slots, rows, far_down, term_out, term_in, pre_gate, pre_up,
    raw_send, raw_recv, own_sem, send_sem, recv_sem, fsend_sem, frecv_sem,
    dsend_sem, drecv_sem, tsend_sem, trecv_sem,
):
    half = experts // 2
    me = lax.axis_index("expert")
    part = lax.axis_index("split")
    base = (me // half) * half
    mine = me - base
    partner = lax.rem(me + half, experts)
    count, width = tok_ref.shape
    capacity = rows.shape[1]
    turns = range(1, splits)
    peer = near(half)

    def cols(which):
        return pl.ds(pl.multiple_of(which * width, width), width)

    def ahead(turn):
        return lax.rem(part + turn, splits)

    def behind(turn):
        return lax.rem(part - turn + splits, splits)

    def raw(k):
        src = (place_ref, prob_ref, tok_ref, grad_ref)[k]
        dst = (far_place, far_prob, far_tok, far_grad)[k]
        return remote(src, dst, raw_send.at[k], raw_recv.at[k], "expert", partner)

    def down(turn):
        return remote(
            down_ref.at[:, cols(ahead(turn))], far_down.at[turn],
            dsend_sem.at[turn], drecv_sem.at[turn], "split", ahead(turn),
        )

    def make(arr, blk, e):
        place = far_place if blk else place_ref
        prob = far_prob if blk else prob_ref
        source = ((tok_ref, far_tok), (grad_ref, far_grad))[arr][blk]
        slot = lax.broadcasted_iota(jnp.int32, (capacity, count), 0) + e * capacity
        first, second = slot == place[0:1, :], slot == place[1:2, :]
        pick = jnp.where(first | second, 1.0, 0.0).astype(jnp.bfloat16)
        value = jnp.dot(pick, source[...], preferred_element_type=jnp.float32)
        if arr == 1:
            scale = jnp.where(first, prob[0:1, :], 0.0) + jnp.where(second, prob[1:2, :], 0.0)
            value = value * jnp.sum(scale, axis=1, keepdims=True)
        return value.astype(jnp.bfloat16)

    def landing(arr, s):
        return in_ref.at[s, :, cols(part)] if arr == 0 else rows.at[s]

    def hop(arr, blk, e, s):
        return remote(
            slots.at[arr, blk, e - base], landing(arr, s), send_sem.at[arr, blk, e - base],
            recv_sem.at[arr, s], "expert", e,
        )

    def pass_on(block, s, turn, frm):
        return remote(
            block, in_ref.at[s, :, cols(frm)], fsend_sem.at[turn, s], frecv_sem.at[turn, s],
            "split", ahead(turn),
        )

    def term(s, turn):
        return remote(
            term_out.at[turn, s], term_in.at[turn, s], tsend_sem.at[turn, s], trecv_sem.at[turn, s],
            "split", behind(turn),
        )

    def keep(blk, s):
        return pltpu.make_async_copy(slots.at[0, blk, mine], in_ref.at[s, :, cols(part)], own_sem.at[blk])

    def over(n0, n1, body):
        def run(i, carry):
            body(i)
            return carry

        lax.fori_loop(n0, n1, run, 0)

    def send_rows(arr, blk):
        s = partner if blk else me

        def one(step):
            e = peer(step)
            slots[arr, blk, e - base] = make(arr, blk, e)
            hop(arr, blk, e, s).start()

        over(1, half, one)
        if arr == 0:
            slots[0, blk, mine] = make(0, blk, me)
            keep(blk, s).start()
            for turn in turns:
                pass_on(slots.at[0, blk, mine], s, turn, part).start()
        else:
            rows[s] = make(1, blk, me)

    def other(step, blk):
        e = peer(half - step)
        return lax.rem(e + half, experts) if blk else e

    def forward(blk):
        def one(step):
            s = other(step, blk)
            hop(0, blk, peer(half - step), s).wait_recv()
            for turn in turns:
                pass_on(in_ref.at[s, :, cols(part)], s, turn, part).start()

        over(1, half, one)

    def terms(s):
        for turn in turns:
            value = lax.dot_general(
                rows[s], far_down[turn], (((1,), (1,)), ((), ())), preferred_element_type=jnp.float32
            )
            term_out[turn, s] = value.astype(jnp.bfloat16)
            term(s, turn).start()

    def use(blk):
        terms(partner if blk else me)

        def one(step):
            s = other(step, blk)
            hop(1, blk, peer(half - step), s).wait_recv()
            terms(s)

        over(1, half, one)

    barrier = pltpu.get_barrier_semaphore()
    over(1, half, lambda step: pl.semaphore_signal(
        barrier, inc=1, device_id={"expert": peer(step)}, device_id_type=MESH))
    pl.semaphore_signal(barrier, inc=1, device_id={"expert": partner}, device_id_type=MESH)
    for turn in turns:
        pl.semaphore_signal(barrier, inc=1, device_id={"split": ahead(turn)}, device_id_type=MESH)
    pl.semaphore_wait(barrier, half - 1 + 1 + splits - 1)

    for k in range(4):
        raw(k).start()
    send_rows(0, 0)
    for turn in turns:
        down(turn).start()
    send_rows(1, 0)
    forward(0)
    for k in range(3):
        raw(k).wait_recv()
    send_rows(0, 1)
    for turn in turns:
        down(turn).wait_recv()
    use(0)
    def project(s):
        for turn in turns:
            pass_on(slots.at[0, 0, 0], s, turn, behind(turn)).wait_recv()
        pre_gate[s] = jnp.dot(in_ref[s], gate_ref[...], preferred_element_type=jnp.float32)
        pre_up[s] = jnp.dot(in_ref[s], up_ref[...], preferred_element_type=jnp.float32)

    raw(3).wait_recv()
    send_rows(1, 1)
    forward(1)
    keep(0, me).wait()
    over(0, half, lambda step: project(peer(half - step)))
    use(1)
    keep(1, partner).wait()
    over(0, half, lambda step: project(lax.rem(peer(half - step) + half, experts)))

    def finish(s):
        value = lax.dot_general(
            rows[s], down_ref[:, cols(part)], (((1,), (1,)), ((), ())),
            preferred_element_type=jnp.float32,
        )
        for turn in turns:
            term(s, turn).wait_recv()
            value = value + term_in[turn, s].astype(jnp.float32)
        gate_pre = pre_gate[s]
        sigmoid_gate = jax.nn.sigmoid(gate_pre)
        dup_ref[s] = (value * (gate_pre * sigmoid_gate)).astype(jnp.bfloat16)
        slope = sigmoid_gate * (1.0 + gate_pre * (1.0 - sigmoid_gate))
        dgate_ref[s] = (value * pre_up[s] * slope).astype(jnp.bfloat16)

    over(0, half, lambda step: finish(peer(half - step)))
    over(0, half, lambda step: finish(lax.rem(peer(half - step) + half, experts)))

    def drain(s):
        for turn in turns:
            term(s, turn).wait_send()
            pass_on(slots.at[0, 0, 0], s, turn, behind(turn)).wait_send()

    over(0, experts, drain)
    for blk in range(2):
        for arr in range(2):
            over(1, half, lambda step: hop(arr, blk, peer(step), me).wait_send())
    for k in range(4):
        raw(k).wait_send()
    for turn in turns:
        down(turn).wait_send()


def dispatch(place, probs, tokens, grads, down_w, gate_w, up_w, experts, splits, capacity):
    count, width = tokens.shape
    hidden = down_w.shape[0]
    half, turns = experts // 2, max(splits, 2)
    bf16, dma = jnp.bfloat16, pltpu.SemaphoreType.DMA
    inside = pl.BlockSpec(memory_space=pltpu.VMEM)
    return pl.pallas_call(
        functools.partial(dispatch_kernel, experts, splits),
        out_shape=(
            jax.ShapeDtypeStruct((experts, capacity, splits * width), bf16),
            jax.ShapeDtypeStruct((experts, capacity, hidden), bf16),
            jax.ShapeDtypeStruct((experts, capacity, hidden), bf16),
        ),
        in_specs=[inside] * 7,
        out_specs=(inside,) * 3,
        scratch_shapes=[
            pltpu.VMEM(place.shape, jnp.int32),
            pltpu.VMEM(probs.shape, jnp.float32),
            pltpu.VMEM((count, width), bf16),
            pltpu.VMEM((count, width), bf16),
            pltpu.VMEM((2, 2, half, capacity, width), bf16),
            pltpu.VMEM((experts, capacity, width), bf16),
            pltpu.VMEM((turns, hidden, width), bf16),
            pltpu.VMEM((turns, experts, capacity, hidden), bf16),
            pltpu.VMEM((turns, experts, capacity, hidden), bf16),
            pltpu.VMEM((experts, capacity, hidden), jnp.float32),
            pltpu.VMEM((experts, capacity, hidden), jnp.float32),
            dma((4,)),
            dma((4,)),
            dma((2,)),
            dma((2, 2, half)),
            dma((2, experts)),
            dma((turns, experts)),
            dma((turns, experts)),
            dma((turns,)),
            dma((turns,)),
            dma((turns, experts)),
            dma((turns, experts)),
        ],
        compiler_params=pltpu.CompilerParams(
            collective_id=0, has_side_effects=True, vmem_limit_bytes=40 << 20
        ),
        name="dispatch",
    )(place, probs, tokens, grads, down_w, gate_w, up_w)


def back_kernel(
    experts, splits, replicas, dgate_ref, dup_ref, gate_ref, up_ref, a_ref, b_ref, c_ref, d_ref,
    home_ref, oa_ref, ob_ref, oc_ref, od_ref,
    away, landed, ready, xsend, xrecv, own_sem, send_sem, recv_sem, rsend, rrecv,
):
    me = lax.axis_index("expert")
    part = lax.axis_index("split")
    copy_of = lax.axis_index("replica")
    width = gate_ref.shape[0] // splits
    stepped = (a_ref, b_ref, c_ref, d_ref)
    others = (oa_ref, ob_ref, oc_ref, od_ref)

    def product(e, which):
        rows = pl.ds(pl.multiple_of(which * width, width), width)
        dims = (((1,), (1,)), ((), ()))
        return lax.dot_general(
            dgate_ref[e], gate_ref[rows, :], dims, preferred_element_type=jnp.float32
        ) + lax.dot_general(dup_ref[e], up_ref[rows, :], dims, preferred_element_type=jnp.float32)

    def swap(k, turn):
        return remote(
            stepped[k], others[k].at[turn - 1], rsend.at[k, turn], rrecv.at[k, turn],
            "replica", lax.rem(copy_of + turn, replicas),
        )

    def cross(e, turn):
        return remote(
            away.at[turn, e], landed.at[turn, e], xsend.at[turn, e], xrecv.at[turn, e],
            "split", lax.rem(part + turn, splits),
        )

    def hop(e, frm):
        return remote(ready.at[e], home_ref.at[frm], send_sem.at[e], recv_sem.at[frm], "expert", e)

    greet((("expert", experts), ("split", splits), ("replica", replicas)))

    def first(step, carry):
        e = lax.rem(me + step, experts)
        for turn in range(1, splits):
            away[turn, e] = product(e, lax.rem(part + turn, splits)).astype(jnp.bfloat16)
            cross(e, turn).start()
        return carry

    lax.fori_loop(1, experts + 1, first, 0)
    for k in range(4):
        for turn in range(1, replicas):
            swap(k, turn).start()

    def total(e):
        value = product(e, part)
        for turn in range(1, splits):
            cross(e, turn).wait_recv()
            value = value + landed[turn, e].astype(jnp.float32)
        ready[e] = value.astype(jnp.bfloat16)

    def second(step, carry):
        e = lax.rem(me + step, experts)
        total(e)
        hop(e, me).start()
        return carry

    lax.fori_loop(1, experts, second, 0)
    total(me)
    keep = pltpu.make_async_copy(ready.at[me], home_ref.at[me], own_sem.at[0])
    keep.start()

    def last(step, carry):
        hop(lax.rem(me + step, experts), me).wait_send()
        s = lax.rem(me - step + experts, experts)
        hop(s, s).wait_recv()
        return carry

    lax.fori_loop(1, experts, last, 0)

    def sent(e, carry):
        for turn in range(1, splits):
            cross(e, turn).wait_send()
        return carry

    lax.fori_loop(0, experts, sent, 0)
    keep.wait()
    for k in range(4):
        for turn in range(1, replicas):
            swap(k, turn).wait()


def send_back(d_gate, d_up, gate_w, up_w, stepped, experts, splits, replicas):
    capacity = d_gate.shape[1]
    width = gate_w.shape[0] // splits
    turns, copies = max(splits, 2), max(replicas, 2)
    held = jax.ShapeDtypeStruct((copies - 1,) + stepped[0].shape, jnp.bfloat16)
    anywhere = pl.BlockSpec(memory_space=pl.ANY)
    inside = pl.BlockSpec(memory_space=pltpu.VMEM)
    return pl.pallas_call(
        functools.partial(back_kernel, experts, splits, replicas),
        out_shape=(jax.ShapeDtypeStruct((experts, capacity, width), jnp.bfloat16),) + (held,) * 4,
        in_specs=[inside] * 4 + [anywhere] * 4,
        out_specs=(anywhere,) * 5,
        scratch_shapes=[
            pltpu.VMEM((turns, experts, capacity, width), jnp.bfloat16),
            pltpu.VMEM((turns, experts, capacity, width), jnp.bfloat16),
            pltpu.VMEM((experts, capacity, width), jnp.bfloat16),
            pltpu.SemaphoreType.DMA((turns, experts)),
            pltpu.SemaphoreType.DMA((turns, experts)),
            pltpu.SemaphoreType.DMA((1,)),
            pltpu.SemaphoreType.DMA((experts,)),
            pltpu.SemaphoreType.DMA((experts,)),
            pltpu.SemaphoreType.DMA((4, copies)),
            pltpu.SemaphoreType.DMA((4, copies)),
        ],
        compiler_params=pltpu.CompilerParams(
            collective_id=1, has_side_effects=True, vmem_limit_bytes=40 << 20
        ),
        name="send_back",
    )(d_gate, d_up, gate_w, up_w, *stepped)


def per_device(tokens, grad_out, expert_ids, route_probs, w_gate, w_up, w_down, mom_gate, mom_up):
    experts, splits = lax.axis_size("expert"), lax.axis_size("split")
    replicas = lax.axis_size("replica")
    tok_count = tokens.shape[1]
    capacity = 4 * tok_count // experts
    targets = slot_targets(expert_ids[0], experts, capacity).reshape(tok_count, 2)
    slot = jnp.arange(experts * capacity, dtype=jnp.int32)
    hits = [slot[:, None] == targets[:, k][None, :] for k in range(2)]
    pick = (hits[0] | hits[1]).astype(jnp.bfloat16)
    probs = route_probs[0]
    place = jnp.pad(targets.T, ((0, 6), (0, 0)))
    gate_local = w_gate[0, 0]
    up_local = w_up[0, 0]
    recv_in, d_gate, d_up = dispatch(
        place, jnp.pad(probs.T, ((0, 6), (0, 0))), tokens[0], grad_out[0], w_down[0, 0],
        gate_local, up_local, experts, splits, capacity,
    )
    row_count = experts * capacity
    dims = (((0,), (0,)), ((), ()))
    rows_in = recv_in.reshape(row_count, -1)
    g_gate = lax.dot_general(
        rows_in, d_gate.reshape(row_count, -1), dims, preferred_element_type=jnp.float32
    )
    g_up = lax.dot_general(
        rows_in, d_up.reshape(row_count, -1), dims, preferred_element_type=jnp.float32
    )
    m_gate = momentum_decay * mom_gate[0, 0].astype(jnp.float32) + g_gate
    m_up = momentum_decay * mom_up[0, 0].astype(jnp.float32) + g_up
    stepped = (
        (gate_local.astype(jnp.float32) - step_size * m_gate).astype(jnp.bfloat16),
        (up_local.astype(jnp.float32) - step_size * m_up).astype(jnp.bfloat16),
        m_gate.astype(jnp.bfloat16),
        m_up.astype(jnp.bfloat16),
    )
    returned, *others = send_back(
        d_gate, d_up, gate_local, up_local,
        stepped, experts, splits, replicas,
    )
    averaged = []
    for mine, rest in zip(stepped, others):
        total = mine.astype(jnp.float32)
        for turn in range(replicas - 1):
            total = total + rest[turn].astype(jnp.float32)
        averaged.append((total / replicas).astype(jnp.bfloat16)[None])
    d_toks = lax.dot_general(
        pick, returned.reshape(row_count, -1), (((0,), (0,)), ((), ())),
        preferred_element_type=jnp.float32,
    ).astype(jnp.bfloat16)
    return (averaged[0], averaged[1], averaged[2], averaged[3], d_toks[None])


def solution(mesh):
    return jax.shard_map(
        per_device,
        mesh=mesh,
        in_specs=(
            P("replica", "expert", "split"),
            P("replica", "expert", "split"),
            P("replica", "expert", None),
            P("replica", "expert", None),
            P("replica", "expert", None, "split"),
            P("replica", "expert", None, "split"),
            P("replica", "expert", "split", None),
            P("replica", "expert", None, "split"),
            P("replica", "expert", None, "split"),
        ),
        out_specs=(
            P("expert", None, "split"),
            P("expert", None, "split"),
            P("expert", None, "split"),
            P("expert", None, "split"),
            P("replica", "expert", "split"),
        ),
        check_vma=False,
    )
```

```python
import functools

import jax
import jax.numpy as jnp
from jax import lax
from jax.experimental import pallas as pl
from jax.experimental.pallas import tpu as pltpu
from jax.sharding import PartitionSpec as P

momentum_decay = 0.9
step_size = 0.005
MESH = pl.DeviceIdType.MESH


def slot_targets(ids_block, experts, capacity):
    flat_ids = ids_block.reshape(-1)
    count = flat_ids.shape[0]
    place = jnp.arange(count, dtype=jnp.int32)
    same = (flat_ids[:, None] == flat_ids[None, :]) & (place[None, :] < place[:, None])
    return flat_ids * capacity + jnp.sum(same.astype(jnp.int32), axis=1)


def greet(axes):
    barrier = pltpu.get_barrier_semaphore()
    total = 0
    for name, size in axes:
        here = lax.axis_index(name)

        def signal(step, carry, name=name, size=size, here=here):
            pl.semaphore_signal(
                barrier, inc=1, device_id={name: lax.rem(here + step, size)}, device_id_type=MESH
            )
            return carry

        lax.fori_loop(1, size, signal, 0)
        total += size - 1
    pl.semaphore_wait(barrier, total)


def remote(src, dst, send, recv, name, to):
    return pltpu.make_async_remote_copy(
        src_ref=src, dst_ref=dst, send_sem=send, recv_sem=recv, device_id={name: to}, device_id_type=MESH
    )


def near(half):
    me = lax.axis_index("expert")
    base = (me // half) * half
    return lambda step: base + lax.rem(me - base + step, half)


def dispatch_kernel(
    experts, splits, place_ref, prob_ref, tok_hbm, grad_hbm, down_hbm, gate_hbm, up_hbm,
    in_ref, dgate_ref, dup_ref,
    far_place, far_prob, far_tok, far_grad, slots, rows, far_down, term_out, term_in, pre_gate, pre_up,
    tok_ref, grad_ref, down_ref, gate_ref, up_ref, load_sem,
    raw_send, raw_recv, own_sem, send_sem, recv_sem, fsend_sem, frecv_sem,
    dsend_sem, drecv_sem, tsend_sem, trecv_sem,
):
    half = experts // 2
    me = lax.axis_index("expert")
    part = lax.axis_index("split")
    base = (me // half) * half
    mine = me - base
    partner = lax.rem(me + half, experts)
    count, width = tok_ref.shape
    capacity = rows.shape[1]
    turns = range(1, splits)
    peer = near(half)

    def cols(which):
        return pl.ds(pl.multiple_of(which * width, width), width)

    def ahead(turn):
        return lax.rem(part + turn, splits)

    def behind(turn):
        return lax.rem(part - turn + splits, splits)

    def load(k):
        src = (tok_hbm, grad_hbm, down_hbm, gate_hbm, up_hbm)[k]
        dst = (tok_ref, grad_ref, down_ref, gate_ref, up_ref)[k]
        return pltpu.make_async_copy(src, dst, load_sem.at[k])

    def raw(k):
        src = (place_ref, prob_ref, tok_hbm, grad_hbm)[k]
        dst = (far_place, far_prob, far_tok, far_grad)[k]
        return remote(src, dst, raw_send.at[k], raw_recv.at[k], "expert", partner)

    def down(turn):
        return remote(
            down_hbm.at[:, cols(ahead(turn))], far_down.at[turn],
            dsend_sem.at[turn], drecv_sem.at[turn], "split", ahead(turn),
        )

    def make(arr, blk, e):
        place = far_place if blk else place_ref
        prob = far_prob if blk else prob_ref
        source = ((tok_ref, far_tok), (grad_ref, far_grad))[arr][blk]
        slot = lax.broadcasted_iota(jnp.int32, (capacity, count), 0) + e * capacity
        first, second = slot == place[0:1, :], slot == place[1:2, :]
        pick = jnp.where(first | second, 1.0, 0.0).astype(jnp.bfloat16)
        value = jnp.dot(pick, source[...], preferred_element_type=jnp.float32)
        if arr == 1:
            scale = jnp.where(first, prob[0:1, :], 0.0) + jnp.where(second, prob[1:2, :], 0.0)
            value = value * jnp.sum(scale, axis=1, keepdims=True)
        return value.astype(jnp.bfloat16)

    def landing(arr, s):
        return in_ref.at[s, :, cols(part)] if arr == 0 else rows.at[s]

    def hop(arr, blk, e, s):
        return remote(
            slots.at[arr, blk, e - base], landing(arr, s), send_sem.at[arr, blk, e - base],
            recv_sem.at[arr, s], "expert", e,
        )

    def pass_on(block, s, turn, frm):
        return remote(
            block, in_ref.at[s, :, cols(frm)], fsend_sem.at[turn, s], frecv_sem.at[turn, s],
            "split", ahead(turn),
        )

    def term(s, turn):
        return remote(
            term_out.at[turn, s], term_in.at[turn, s], tsend_sem.at[turn, s], trecv_sem.at[turn, s],
            "split", behind(turn),
        )

    def keep(blk, s):
        return pltpu.make_async_copy(slots.at[0, blk, mine], in_ref.at[s, :, cols(part)], own_sem.at[blk])

    def over(n0, n1, body):
        def run(i, carry):
            body(i)
            return carry

        lax.fori_loop(n0, n1, run, 0)

    def send_rows(arr, blk):
        s = partner if blk else me

        def one(step):
            e = peer(step)
            slots[arr, blk, e - base] = make(arr, blk, e)
            hop(arr, blk, e, s).start()

        over(1, half, one)
        if arr == 0:
            slots[0, blk, mine] = make(0, blk, me)
            keep(blk, s).start()
            for turn in turns:
                pass_on(slots.at[0, blk, mine], s, turn, part).start()
        else:
            rows[s] = make(1, blk, me)

    def other(step, blk):
        e = peer(half - step)
        return lax.rem(e + half, experts) if blk else e

    def forward(blk):
        def one(step):
            s = other(step, blk)
            hop(0, blk, peer(half - step), s).wait_recv()
            for turn in turns:
                pass_on(in_ref.at[s, :, cols(part)], s, turn, part).start()

        over(1, half, one)

    def terms(s):
        for turn in turns:
            value = lax.dot_general(
                rows[s], far_down[turn], (((1,), (1,)), ((), ())), preferred_element_type=jnp.float32
            )
            term_out[turn, s] = value.astype(jnp.bfloat16)
            term(s, turn).start()

    def use(blk):
        terms(partner if blk else me)

        def one(step):
            s = other(step, blk)
            hop(1, blk, peer(half - step), s).wait_recv()
            terms(s)

        over(1, half, one)

    for k in range(5):
        load(k).start()
    barrier = pltpu.get_barrier_semaphore()
    over(1, half, lambda step: pl.semaphore_signal(
        barrier, inc=1, device_id={"expert": peer(step)}, device_id_type=MESH))
    pl.semaphore_signal(barrier, inc=1, device_id={"expert": partner}, device_id_type=MESH)
    for turn in turns:
        pl.semaphore_signal(barrier, inc=1, device_id={"split": ahead(turn)}, device_id_type=MESH)
    pl.semaphore_wait(barrier, half - 1 + 1 + splits - 1)

    for k in range(3):
        raw(k).start()
    load(0).wait()
    send_rows(0, 0)
    for turn in turns:
        down(turn).start()
    load(1).wait()
    send_rows(1, 0)
    forward(0)
    for k in range(3):
        raw(k).wait_recv()
    raw(3).start()
    send_rows(0, 1)
    for turn in turns:
        down(turn).wait_recv()
    use(0)
    def project(s):
        for turn in turns:
            pass_on(slots.at[0, 0, 0], s, turn, behind(turn)).wait_recv()
        pre_gate[s] = jnp.dot(in_ref[s], gate_ref[...], preferred_element_type=jnp.float32)
        pre_up[s] = jnp.dot(in_ref[s], up_ref[...], preferred_element_type=jnp.float32)

    raw(3).wait_recv()
    send_rows(1, 1)
    forward(1)
    for k in range(2, 5):
        load(k).wait()
    keep(0, me).wait()
    over(0, half, lambda step: project(peer(half - step)))
    use(1)
    keep(1, partner).wait()
    over(0, half, lambda step: project(lax.rem(peer(half - step) + half, experts)))

    def finish(s):
        value = lax.dot_general(
            rows[s], down_ref[:, cols(part)], (((1,), (1,)), ((), ())),
            preferred_element_type=jnp.float32,
        )
        for turn in turns:
            term(s, turn).wait_recv()
            value = value + term_in[turn, s].astype(jnp.float32)
        gate_pre = pre_gate[s]
        sigmoid_gate = jax.nn.sigmoid(gate_pre)
        dup_ref[s] = (value * (gate_pre * sigmoid_gate)).astype(jnp.bfloat16)
        slope = sigmoid_gate * (1.0 + gate_pre * (1.0 - sigmoid_gate))
        dgate_ref[s] = (value * pre_up[s] * slope).astype(jnp.bfloat16)

    over(0, half, lambda step: finish(peer(half - step)))
    over(0, half, lambda step: finish(lax.rem(peer(half - step) + half, experts)))

    def drain(s):
        for turn in turns:
            term(s, turn).wait_send()
            pass_on(slots.at[0, 0, 0], s, turn, behind(turn)).wait_send()

    over(0, experts, drain)
    for blk in range(2):
        for arr in range(2):
            over(1, half, lambda step: hop(arr, blk, peer(step), me).wait_send())
    for k in range(4):
        raw(k).wait_send()
    for turn in turns:
        down(turn).wait_send()


def dispatch(place, probs, tokens, grads, down_w, gate_w, up_w, experts, splits, capacity):
    count, width = tokens.shape
    hidden = down_w.shape[0]
    half, turns = experts // 2, max(splits, 2)
    bf16, dma = jnp.bfloat16, pltpu.SemaphoreType.DMA
    inside = pl.BlockSpec(memory_space=pltpu.VMEM)
    return pl.pallas_call(
        functools.partial(dispatch_kernel, experts, splits),
        out_shape=(
            jax.ShapeDtypeStruct((experts, capacity, splits * width), bf16),
            jax.ShapeDtypeStruct((experts, capacity, hidden), bf16),
            jax.ShapeDtypeStruct((experts, capacity, hidden), bf16),
        ),
        in_specs=[inside] * 2 + [pl.BlockSpec(memory_space=pltpu.HBM)] * 5,
        out_specs=(inside,) * 3,
        scratch_shapes=[
            pltpu.VMEM(place.shape, jnp.int32),
            pltpu.VMEM(probs.shape, jnp.float32),
            pltpu.VMEM((count, width), bf16),
            pltpu.VMEM((count, width), bf16),
            pltpu.VMEM((2, 2, half, capacity, width), bf16),
            pltpu.VMEM((experts, capacity, width), bf16),
            pltpu.VMEM((turns, hidden, width), bf16),
            pltpu.VMEM((turns, experts, capacity, hidden), bf16),
            pltpu.VMEM((turns, experts, capacity, hidden), bf16),
            pltpu.VMEM((experts, capacity, hidden), jnp.float32),
            pltpu.VMEM((experts, capacity, hidden), jnp.float32),
            pltpu.VMEM((count, width), bf16),
            pltpu.VMEM((count, width), bf16),
            pltpu.VMEM(down_w.shape, bf16),
            pltpu.VMEM(gate_w.shape, bf16),
            pltpu.VMEM(up_w.shape, bf16),
            dma((5,)),
            dma((4,)),
            dma((4,)),
            dma((2,)),
            dma((2, 2, half)),
            dma((2, experts)),
            dma((turns, experts)),
            dma((turns, experts)),
            dma((turns,)),
            dma((turns,)),
            dma((turns, experts)),
            dma((turns, experts)),
        ],
        compiler_params=pltpu.CompilerParams(
            collective_id=0, has_side_effects=True, vmem_limit_bytes=40 << 20
        ),
        name="dispatch",
    )(place, probs, tokens, grads, down_w, gate_w, up_w)


def back_kernel(
    experts, splits, replicas, dgate_ref, dup_ref, gate_ref, up_ref, a_ref, b_ref, c_ref, d_ref,
    home_ref, oa_ref, ob_ref, oc_ref, od_ref,
    away, landed, ready, xsend, xrecv, own_sem, send_sem, recv_sem, rsend, rrecv,
):
    me = lax.axis_index("expert")
    part = lax.axis_index("split")
    copy_of = lax.axis_index("replica")
    width = gate_ref.shape[0] // splits
    stepped = (a_ref, b_ref, c_ref, d_ref)
    others = (oa_ref, ob_ref, oc_ref, od_ref)

    def product(e, which):
        rows = pl.ds(pl.multiple_of(which * width, width), width)
        dims = (((1,), (1,)), ((), ()))
        return lax.dot_general(
            dgate_ref[e], gate_ref[rows, :], dims, preferred_element_type=jnp.float32
        ) + lax.dot_general(dup_ref[e], up_ref[rows, :], dims, preferred_element_type=jnp.float32)

    def swap(k, turn):
        return remote(
            stepped[k], others[k].at[turn - 1], rsend.at[k, turn], rrecv.at[k, turn],
            "replica", lax.rem(copy_of + turn, replicas),
        )

    def cross(e, turn):
        return remote(
            away.at[turn, e], landed.at[turn, e], xsend.at[turn, e], xrecv.at[turn, e],
            "split", lax.rem(part + turn, splits),
        )

    def hop(e, frm):
        return remote(ready.at[e], home_ref.at[frm], send_sem.at[e], recv_sem.at[frm], "expert", e)

    greet((("expert", experts), ("split", splits), ("replica", replicas)))

    half = experts // 2
    peer = near(half)

    def order(step):
        return lax.rem(peer(lax.rem(step, half)) + half * (1 - step // half), experts)

    def first(step, carry):
        e = order(step)
        for turn in range(1, splits):
            away[turn, e] = product(e, lax.rem(part + turn, splits)).astype(jnp.bfloat16)
            cross(e, turn).start()
        return carry

    lax.fori_loop(0, half, first, 0)
    lax.fori_loop(half + 1, experts, first, 0)
    first(half, 0)
    for k in range(4):
        for turn in range(1, replicas):
            swap(k, turn).start()

    def total(e):
        value = product(e, part)
        for turn in range(1, splits):
            cross(e, turn).wait_recv()
            value = value + landed[turn, e].astype(jnp.float32)
        ready[e] = value.astype(jnp.bfloat16)

    def second(step, carry):
        e = order(step)
        total(e)
        hop(e, me).start()
        return carry

    lax.fori_loop(0, half, second, 0)
    lax.fori_loop(half + 1, experts, second, 0)
    total(me)
    keep = pltpu.make_async_copy(ready.at[me], home_ref.at[me], own_sem.at[0])
    keep.start()

    def last(step, carry):
        hop(lax.rem(me + step, experts), me).wait_send()
        s = lax.rem(me - step + experts, experts)
        hop(s, s).wait_recv()
        return carry

    lax.fori_loop(1, experts, last, 0)

    def sent(e, carry):
        for turn in range(1, splits):
            cross(e, turn).wait_send()
        return carry

    lax.fori_loop(0, experts, sent, 0)
    keep.wait()
    for k in range(4):
        for turn in range(1, replicas):
            swap(k, turn).wait()


def send_back(d_gate, d_up, gate_w, up_w, stepped, experts, splits, replicas):
    capacity = d_gate.shape[1]
    width = gate_w.shape[0] // splits
    turns, copies = max(splits, 2), max(replicas, 2)
    held = jax.ShapeDtypeStruct((copies - 1,) + stepped[0].shape, jnp.bfloat16)
    anywhere = pl.BlockSpec(memory_space=pl.ANY)
    inside = pl.BlockSpec(memory_space=pltpu.VMEM)
    return pl.pallas_call(
        functools.partial(back_kernel, experts, splits, replicas),
        out_shape=(jax.ShapeDtypeStruct((experts, capacity, width), jnp.bfloat16),) + (held,) * 4,
        in_specs=[inside] * 4 + [anywhere] * 4,
        out_specs=(anywhere,) * 5,
        scratch_shapes=[
            pltpu.VMEM((turns, experts, capacity, width), jnp.bfloat16),
            pltpu.VMEM((turns, experts, capacity, width), jnp.bfloat16),
            pltpu.VMEM((experts, capacity, width), jnp.bfloat16),
            pltpu.SemaphoreType.DMA((turns, experts)),
            pltpu.SemaphoreType.DMA((turns, experts)),
            pltpu.SemaphoreType.DMA((1,)),
            pltpu.SemaphoreType.DMA((experts,)),
            pltpu.SemaphoreType.DMA((experts,)),
            pltpu.SemaphoreType.DMA((4, copies)),
            pltpu.SemaphoreType.DMA((4, copies)),
        ],
        compiler_params=pltpu.CompilerParams(
            collective_id=1, has_side_effects=True, vmem_limit_bytes=40 << 20
        ),
        name="send_back",
    )(d_gate, d_up, gate_w, up_w, *stepped)


def per_device(tokens, grad_out, expert_ids, route_probs, w_gate, w_up, w_down, mom_gate, mom_up):
    experts, splits = lax.axis_size("expert"), lax.axis_size("split")
    replicas = lax.axis_size("replica")
    tok_count = tokens.shape[1]
    capacity = 4 * tok_count // experts
    targets = slot_targets(expert_ids[0], experts, capacity).reshape(tok_count, 2)
    slot = jnp.arange(experts * capacity, dtype=jnp.int32)
    hits = [slot[:, None] == targets[:, k][None, :] for k in range(2)]
    pick = (hits[0] | hits[1]).astype(jnp.bfloat16)
    probs = route_probs[0]
    place = jnp.pad(targets.T, ((0, 6), (0, 0)))
    gate_local = w_gate[0, 0]
    up_local = w_up[0, 0]
    recv_in, d_gate, d_up = dispatch(
        place, jnp.pad(probs.T, ((0, 6), (0, 0))), tokens[0], grad_out[0], w_down[0, 0],
        gate_local, up_local, experts, splits, capacity,
    )
    row_count = experts * capacity
    dims = (((0,), (0,)), ((), ()))
    rows_in = recv_in.reshape(row_count, -1)
    g_gate = lax.dot_general(
        rows_in, d_gate.reshape(row_count, -1), dims, preferred_element_type=jnp.float32
    )
    g_up = lax.dot_general(
        rows_in, d_up.reshape(row_count, -1), dims, preferred_element_type=jnp.float32
    )
    m_gate = momentum_decay * mom_gate[0, 0].astype(jnp.float32) + g_gate
    m_up = momentum_decay * mom_up[0, 0].astype(jnp.float32) + g_up
    stepped = (
        (gate_local.astype(jnp.float32) - step_size * m_gate).astype(jnp.bfloat16),
        (up_local.astype(jnp.float32) - step_size * m_up).astype(jnp.bfloat16),
        m_gate.astype(jnp.bfloat16),
        m_up.astype(jnp.bfloat16),
    )
    returned, *others = send_back(
        d_gate, d_up, gate_local, up_local,
        stepped, experts, splits, replicas,
    )
    averaged = []
    for mine, rest in zip(stepped, others):
        total = mine.astype(jnp.float32)
        for turn in range(replicas - 1):
            total = total + rest[turn].astype(jnp.float32)
        averaged.append((total / replicas).astype(jnp.bfloat16)[None])
    d_toks = lax.dot_general(
        pick, returned.reshape(row_count, -1), (((0,), (0,)), ((), ())),
        preferred_element_type=jnp.float32,
    ).astype(jnp.bfloat16)
    return (averaged[0], averaged[1], averaged[2], averaged[3], d_toks[None])


def solution(mesh):
    return jax.shard_map(
        per_device,
        mesh=mesh,
        in_specs=(
            P("replica", "expert", "split"),
            P("replica", "expert", "split"),
            P("replica", "expert", None),
            P("replica", "expert", None),
            P("replica", "expert", None, "split"),
            P("replica", "expert", None, "split"),
            P("replica", "expert", "split", None),
            P("replica", "expert", None, "split"),
            P("replica", "expert", None, "split"),
        ),
        out_specs=(
            P("expert", None, "split"),
            P("expert", None, "split"),
            P("expert", None, "split"),
            P("expert", None, "split"),
            P("replica", "expert", "split"),
        ),
        check_vma=False,
    )
```

```python
import functools

import jax
import jax.numpy as jnp
from jax import lax
from jax.experimental import pallas as pl
from jax.experimental.pallas import tpu as pltpu
from jax.sharding import PartitionSpec as P

momentum_decay = 0.9
step_size = 0.005
MESH = pl.DeviceIdType.MESH


def slot_targets(ids_block, experts, capacity):
    flat_ids = ids_block.reshape(-1)
    count = flat_ids.shape[0]
    place = jnp.arange(count, dtype=jnp.int32)
    same = (flat_ids[:, None] == flat_ids[None, :]) & (place[None, :] < place[:, None])
    return flat_ids * capacity + jnp.sum(same.astype(jnp.int32), axis=1)


def greet(axes):
    barrier = pltpu.get_barrier_semaphore()
    total = 0
    for name, size in axes:
        here = lax.axis_index(name)

        def signal(step, carry, name=name, size=size, here=here):
            pl.semaphore_signal(
                barrier, inc=1, device_id={name: lax.rem(here + step, size)}, device_id_type=MESH
            )
            return carry

        lax.fori_loop(1, size, signal, 0)
        total += size - 1
    pl.semaphore_wait(barrier, total)


def remote(src, dst, send, recv, name, to):
    return pltpu.make_async_remote_copy(
        src_ref=src, dst_ref=dst, send_sem=send, recv_sem=recv, device_id={name: to}, device_id_type=MESH
    )


def near(half):
    me = lax.axis_index("expert")
    base = (me // half) * half
    return lambda step: base + lax.rem(me - base + step, half)


def dispatch_kernel(
    experts, splits, place_ref, prob_ref, tok_hbm, grad_hbm, down_hbm, gate_hbm, up_hbm,
    in_ref, dgate_ref, dup_ref,
    far_place, far_prob, far_tok, far_grad, slots, rows, far_down, term_out, term_in, pre_gate, pre_up,
    tok_ref, grad_ref, down_ref, gate_ref, up_ref, load_sem,
    raw_send, raw_recv, own_sem, send_sem, recv_sem, fsend_sem, frecv_sem,
    dsend_sem, drecv_sem, tsend_sem, trecv_sem,
):
    half = experts // 2
    me = lax.axis_index("expert")
    part = lax.axis_index("split")
    base = (me // half) * half
    mine = me - base
    partner = lax.rem(me + half, experts)
    count, width = tok_ref.shape
    capacity = rows.shape[1]
    turns = range(1, splits)
    peer = near(half)

    def cols(which):
        return pl.ds(pl.multiple_of(which * width, width), width)

    def ahead(turn):
        return lax.rem(part + turn, splits)

    def behind(turn):
        return lax.rem(part - turn + splits, splits)

    def load(k):
        src = (tok_hbm, grad_hbm, down_hbm, gate_hbm, up_hbm)[k]
        dst = (tok_ref, grad_ref, down_ref, gate_ref, up_ref)[k]
        return pltpu.make_async_copy(src, dst, load_sem.at[k])

    def raw(k):
        src = (place_ref, prob_ref, tok_hbm, grad_hbm)[k]
        dst = (far_place, far_prob, far_tok, far_grad)[k]
        return remote(src, dst, raw_send.at[k], raw_recv.at[k], "expert", partner)

    def down(turn):
        return remote(
            down_hbm.at[:, cols(ahead(turn))], far_down.at[turn],
            dsend_sem.at[turn], drecv_sem.at[turn], "split", ahead(turn),
        )

    def make(arr, blk, e):
        place = far_place if blk else place_ref
        prob = far_prob if blk else prob_ref
        source = ((tok_ref, far_tok), (grad_ref, far_grad))[arr][blk]
        slot = lax.broadcasted_iota(jnp.int32, (capacity, count), 0) + e * capacity
        first, second = slot == place[0:1, :], slot == place[1:2, :]
        pick = jnp.where(first | second, 1.0, 0.0).astype(jnp.bfloat16)
        value = jnp.dot(pick, source[...], preferred_element_type=jnp.float32)
        if arr == 1:
            scale = jnp.where(first, prob[0:1, :], 0.0) + jnp.where(second, prob[1:2, :], 0.0)
            value = value * jnp.sum(scale, axis=1, keepdims=True)
        return value.astype(jnp.bfloat16)

    def landing(arr, s):
        return in_ref.at[s, :, cols(part)] if arr == 0 else rows.at[s]

    def hop(arr, blk, e, s):
        return remote(
            slots.at[arr, blk, e - base], landing(arr, s), send_sem.at[arr, blk, e - base],
            recv_sem.at[arr, s], "expert", e,
        )

    def pass_on(block, s, turn, frm):
        return remote(
            block, in_ref.at[s, :, cols(frm)], fsend_sem.at[turn, s], frecv_sem.at[turn, s],
            "split", ahead(turn),
        )

    def term(s, turn):
        return remote(
            term_out.at[turn, s], term_in.at[turn, s], tsend_sem.at[turn, s], trecv_sem.at[turn, s],
            "split", behind(turn),
        )

    def keep(blk, s):
        return pltpu.make_async_copy(slots.at[0, blk, mine], in_ref.at[s, :, cols(part)], own_sem.at[blk])

    def over(n0, n1, body):
        def run(i, carry):
            body(i)
            return carry

        lax.fori_loop(n0, n1, run, 0)

    def send_rows(arr, blk):
        s = partner if blk else me

        def one(step):
            e = peer(step)
            slots[arr, blk, e - base] = make(arr, blk, e)
            hop(arr, blk, e, s).start()

        over(1, half, one)
        if arr == 0:
            slots[0, blk, mine] = make(0, blk, me)
            keep(blk, s).start()
            for turn in turns:
                pass_on(slots.at[0, blk, mine], s, turn, part).start()
        else:
            rows[s] = make(1, blk, me)

    def other(step, blk):
        e = peer(half - step)
        return lax.rem(e + half, experts) if blk else e

    def forward(blk):
        def one(step):
            s = other(step, blk)
            hop(0, blk, peer(half - step), s).wait_recv()
            for turn in turns:
                pass_on(in_ref.at[s, :, cols(part)], s, turn, part).start()

        over(1, half, one)

    def terms(s):
        for turn in turns:
            value = lax.dot_general(
                rows[s], far_down[turn], (((1,), (1,)), ((), ())), preferred_element_type=jnp.float32
            )
            term_out[turn, s] = value.astype(jnp.bfloat16)
            term(s, turn).start()

    def use(blk):
        terms(partner if blk else me)

        def one(step):
            s = other(step, blk)
            hop(1, blk, peer(half - step), s).wait_recv()
            terms(s)

        over(1, half, one)

    for k in range(5):
        load(k).start()
    barrier = pltpu.get_barrier_semaphore()
    over(1, half, lambda step: pl.semaphore_signal(
        barrier, inc=1, device_id={"expert": peer(step)}, device_id_type=MESH))
    pl.semaphore_signal(barrier, inc=1, device_id={"expert": partner}, device_id_type=MESH)
    for turn in turns:
        pl.semaphore_signal(barrier, inc=1, device_id={"split": ahead(turn)}, device_id_type=MESH)
    pl.semaphore_wait(barrier, half - 1 + 1 + splits - 1)

    for k in range(3):
        raw(k).start()
    load(0).wait()
    send_rows(0, 0)
    for turn in turns:
        down(turn).start()
    forward(0)
    load(1).wait()
    send_rows(1, 0)
    for k in range(3):
        raw(k).wait_recv()
    raw(3).start()
    send_rows(0, 1)
    for turn in turns:
        down(turn).wait_recv()
    use(0)
    def project(s):
        for turn in turns:
            pass_on(slots.at[0, 0, 0], s, turn, behind(turn)).wait_recv()
        pre_gate[s] = jnp.dot(in_ref[s], gate_ref[...], preferred_element_type=jnp.float32)
        pre_up[s] = jnp.dot(in_ref[s], up_ref[...], preferred_element_type=jnp.float32)

    raw(3).wait_recv()
    send_rows(1, 1)
    forward(1)
    for k in range(2, 5):
        load(k).wait()
    keep(0, me).wait()
    over(0, half, lambda step: project(peer(half - step)))
    use(1)
    keep(1, partner).wait()
    over(0, half, lambda step: project(lax.rem(peer(half - step) + half, experts)))

    def finish(s):
        value = lax.dot_general(
            rows[s], down_ref[:, cols(part)], (((1,), (1,)), ((), ())),
            preferred_element_type=jnp.float32,
        )
        for turn in turns:
            term(s, turn).wait_recv()
            value = value + term_in[turn, s].astype(jnp.float32)
        gate_pre = pre_gate[s]
        sigmoid_gate = jax.nn.sigmoid(gate_pre)
        dup_ref[s] = (value * (gate_pre * sigmoid_gate)).astype(jnp.bfloat16)
        slope = sigmoid_gate * (1.0 + gate_pre * (1.0 - sigmoid_gate))
        dgate_ref[s] = (value * pre_up[s] * slope).astype(jnp.bfloat16)

    over(0, half, lambda step: finish(peer(half - step)))
    over(0, half, lambda step: finish(lax.rem(peer(half - step) + half, experts)))

    def drain(s):
        for turn in turns:
            term(s, turn).wait_send()
            pass_on(slots.at[0, 0, 0], s, turn, behind(turn)).wait_send()

    over(0, experts, drain)
    for blk in range(2):
        for arr in range(2):
            over(1, half, lambda step: hop(arr, blk, peer(step), me).wait_send())
    for k in range(4):
        raw(k).wait_send()
    for turn in turns:
        down(turn).wait_send()


def dispatch(place, probs, tokens, grads, down_w, gate_w, up_w, experts, splits, capacity):
    count, width = tokens.shape
    hidden = down_w.shape[0]
    half, turns = experts // 2, max(splits, 2)
    bf16, dma = jnp.bfloat16, pltpu.SemaphoreType.DMA
    inside = pl.BlockSpec(memory_space=pltpu.VMEM)
    return pl.pallas_call(
        functools.partial(dispatch_kernel, experts, splits),
        out_shape=(
            jax.ShapeDtypeStruct((experts, capacity, splits * width), bf16),
            jax.ShapeDtypeStruct((experts, capacity, hidden), bf16),
            jax.ShapeDtypeStruct((experts, capacity, hidden), bf16),
        ),
        in_specs=[inside] * 2 + [pl.BlockSpec(memory_space=pltpu.HBM)] * 5,
        out_specs=(inside,) * 3,
        scratch_shapes=[
            pltpu.VMEM(place.shape, jnp.int32),
            pltpu.VMEM(probs.shape, jnp.float32),
            pltpu.VMEM((count, width), bf16),
            pltpu.VMEM((count, width), bf16),
            pltpu.VMEM((2, 2, half, capacity, width), bf16),
            pltpu.VMEM((experts, capacity, width), bf16),
            pltpu.VMEM((turns, hidden, width), bf16),
            pltpu.VMEM((turns, experts, capacity, hidden), bf16),
            pltpu.VMEM((turns, experts, capacity, hidden), bf16),
            pltpu.VMEM((experts, capacity, hidden), jnp.float32),
            pltpu.VMEM((experts, capacity, hidden), jnp.float32),
            pltpu.VMEM((count, width), bf16),
            pltpu.VMEM((count, width), bf16),
            pltpu.VMEM(down_w.shape, bf16),
            pltpu.VMEM(gate_w.shape, bf16),
            pltpu.VMEM(up_w.shape, bf16),
            dma((5,)),
            dma((4,)),
            dma((4,)),
            dma((2,)),
            dma((2, 2, half)),
            dma((2, experts)),
            dma((turns, experts)),
            dma((turns, experts)),
            dma((turns,)),
            dma((turns,)),
            dma((turns, experts)),
            dma((turns, experts)),
        ],
        compiler_params=pltpu.CompilerParams(
            collective_id=0, has_side_effects=True, vmem_limit_bytes=40 << 20
        ),
        name="dispatch",
    )(place, probs, tokens, grads, down_w, gate_w, up_w)


def back_kernel(
    experts, splits, replicas, dgate_ref, dup_ref, gate_ref, up_ref, a_ref, b_ref, c_ref, d_ref,
    home_ref, oa_ref, ob_ref, oc_ref, od_ref,
    away, landed, ready, xsend, xrecv, own_sem, send_sem, recv_sem, rsend, rrecv,
):
    me = lax.axis_index("expert")
    part = lax.axis_index("split")
    copy_of = lax.axis_index("replica")
    width = gate_ref.shape[0] // splits
    stepped = (a_ref, b_ref, c_ref, d_ref)
    others = (oa_ref, ob_ref, oc_ref, od_ref)

    def product(e, which):
        rows = pl.ds(pl.multiple_of(which * width, width), width)
        dims = (((1,), (1,)), ((), ()))
        return lax.dot_general(
            dgate_ref[e], gate_ref[rows, :], dims, preferred_element_type=jnp.float32
        ) + lax.dot_general(dup_ref[e], up_ref[rows, :], dims, preferred_element_type=jnp.float32)

    def swap(k, turn):
        return remote(
            stepped[k], others[k].at[turn - 1], rsend.at[k, turn], rrecv.at[k, turn],
            "replica", lax.rem(copy_of + turn, replicas),
        )

    def cross(e, turn):
        return remote(
            away.at[turn, e], landed.at[turn, e], xsend.at[turn, e], xrecv.at[turn, e],
            "split", lax.rem(part + turn, splits),
        )

    def hop(e, frm):
        return remote(ready.at[e], home_ref.at[frm], send_sem.at[e], recv_sem.at[frm], "expert", e)

    greet((("expert", experts), ("split", splits), ("replica", replicas)))

    half = experts // 2
    peer = near(half)

    def order(step):
        return lax.rem(peer(lax.rem(step, half)) + half * (1 - step // half), experts)

    def first(step, carry):
        e = order(step)
        for turn in range(1, splits):
            away[turn, e] = product(e, lax.rem(part + turn, splits)).astype(jnp.bfloat16)
            cross(e, turn).start()
        return carry

    lax.fori_loop(0, half, first, 0)
    lax.fori_loop(half + 1, experts, first, 0)
    first(half, 0)
    for k in range(4):
        for turn in range(1, replicas):
            swap(k, turn).start()

    def total(e):
        value = product(e, part)
        for turn in range(1, splits):
            cross(e, turn).wait_recv()
            value = value + landed[turn, e].astype(jnp.float32)
        ready[e] = value.astype(jnp.bfloat16)

    def second(step, carry):
        e = order(step)
        total(e)
        hop(e, me).start()
        return carry

    lax.fori_loop(0, half, second, 0)
    lax.fori_loop(half + 1, experts, second, 0)
    total(me)
    keep = pltpu.make_async_copy(ready.at[me], home_ref.at[me], own_sem.at[0])
    keep.start()

    def last(step, carry):
        hop(lax.rem(me + step, experts), me).wait_send()
        s = lax.rem(me - step + experts, experts)
        hop(s, s).wait_recv()
        return carry

    lax.fori_loop(1, experts, last, 0)

    def sent(e, carry):
        for turn in range(1, splits):
            cross(e, turn).wait_send()
        return carry

    lax.fori_loop(0, experts, sent, 0)
    keep.wait()
    for k in range(4):
        for turn in range(1, replicas):
            swap(k, turn).wait()


def send_back(d_gate, d_up, gate_w, up_w, stepped, experts, splits, replicas):
    capacity = d_gate.shape[1]
    width = gate_w.shape[0] // splits
    turns, copies = max(splits, 2), max(replicas, 2)
    held = jax.ShapeDtypeStruct((copies - 1,) + stepped[0].shape, jnp.bfloat16)
    anywhere = pl.BlockSpec(memory_space=pl.ANY)
    inside = pl.BlockSpec(memory_space=pltpu.VMEM)
    return pl.pallas_call(
        functools.partial(back_kernel, experts, splits, replicas),
        out_shape=(jax.ShapeDtypeStruct((experts, capacity, width), jnp.bfloat16),) + (held,) * 4,
        in_specs=[inside] * 4 + [anywhere] * 4,
        out_specs=(anywhere,) * 5,
        scratch_shapes=[
            pltpu.VMEM((turns, experts, capacity, width), jnp.bfloat16),
            pltpu.VMEM((turns, experts, capacity, width), jnp.bfloat16),
            pltpu.VMEM((experts, capacity, width), jnp.bfloat16),
            pltpu.SemaphoreType.DMA((turns, experts)),
            pltpu.SemaphoreType.DMA((turns, experts)),
            pltpu.SemaphoreType.DMA((1,)),
            pltpu.SemaphoreType.DMA((experts,)),
            pltpu.SemaphoreType.DMA((experts,)),
            pltpu.SemaphoreType.DMA((4, copies)),
            pltpu.SemaphoreType.DMA((4, copies)),
        ],
        compiler_params=pltpu.CompilerParams(
            collective_id=1, has_side_effects=True, vmem_limit_bytes=40 << 20
        ),
        name="send_back",
    )(d_gate, d_up, gate_w, up_w, *stepped)


def per_device(tokens, grad_out, expert_ids, route_probs, w_gate, w_up, w_down, mom_gate, mom_up):
    experts, splits = lax.axis_size("expert"), lax.axis_size("split")
    replicas = lax.axis_size("replica")
    tok_count = tokens.shape[1]
    capacity = 4 * tok_count // experts
    targets = slot_targets(expert_ids[0], experts, capacity).reshape(tok_count, 2)
    slot = jnp.arange(experts * capacity, dtype=jnp.int32)
    hits = [slot[:, None] == targets[:, k][None, :] for k in range(2)]
    pick = (hits[0] | hits[1]).astype(jnp.bfloat16)
    probs = route_probs[0]
    place = jnp.pad(targets.T, ((0, 6), (0, 0)))
    gate_local = w_gate[0, 0]
    up_local = w_up[0, 0]
    recv_in, d_gate, d_up = dispatch(
        place, jnp.pad(probs.T, ((0, 6), (0, 0))), tokens[0], grad_out[0], w_down[0, 0],
        gate_local, up_local, experts, splits, capacity,
    )
    row_count = experts * capacity
    dims = (((0,), (0,)), ((), ()))
    rows_in = recv_in.reshape(row_count, -1)
    g_gate = lax.dot_general(
        rows_in, d_gate.reshape(row_count, -1), dims, preferred_element_type=jnp.float32
    )
    g_up = lax.dot_general(
        rows_in, d_up.reshape(row_count, -1), dims, preferred_element_type=jnp.float32
    )
    m_gate = momentum_decay * mom_gate[0, 0].astype(jnp.float32) + g_gate
    m_up = momentum_decay * mom_up[0, 0].astype(jnp.float32) + g_up
    stepped = (
        (gate_local.astype(jnp.float32) - step_size * m_gate).astype(jnp.bfloat16),
        (up_local.astype(jnp.float32) - step_size * m_up).astype(jnp.bfloat16),
        m_gate.astype(jnp.bfloat16),
        m_up.astype(jnp.bfloat16),
    )
    returned, *others = send_back(
        d_gate, d_up, gate_local, up_local,
        stepped, experts, splits, replicas,
    )
    averaged = []
    for mine, rest in zip(stepped, others):
        total = mine.astype(jnp.float32)
        for turn in range(replicas - 1):
            total = total + rest[turn].astype(jnp.float32)
        averaged.append((total / replicas).astype(jnp.bfloat16)[None])
    d_toks = lax.dot_general(
        pick, returned.reshape(row_count, -1), (((0,), (0,)), ((), ())),
        preferred_element_type=jnp.float32,
    ).astype(jnp.bfloat16)
    return (averaged[0], averaged[1], averaged[2], averaged[3], d_toks[None])


def solution(mesh):
    return jax.shard_map(
        per_device,
        mesh=mesh,
        in_specs=(
            P("replica", "expert", "split"),
            P("replica", "expert", "split"),
            P("replica", "expert", None),
            P("replica", "expert", None),
            P("replica", "expert", None, "split"),
            P("replica", "expert", None, "split"),
            P("replica", "expert", "split", None),
            P("replica", "expert", None, "split"),
            P("replica", "expert", None, "split"),
        ),
        out_specs=(
            P("expert", None, "split"),
            P("expert", None, "split"),
            P("expert", None, "split"),
            P("expert", None, "split"),
            P("replica", "expert", "split"),
        ),
        check_vma=False,
    )
```
